32 devices in a mesh: heads: 8 (over z, y), hid: 4 (over x, core).
Axes of the slice: x: 2, y: 2, z: 4, core: 2. Of those that a mesh axis runs over, the one named last changes fastest.
Arguments:
- inputs: bfloat16 [8192, 1024], P(('hid', 'heads')), may hold values from -6 to 6
- cotangent: bfloat16 [8192, 1024], P(('hid', 'heads')), may hold values from -6 to 6
- segments: int32 [8192], P(('hid', 'heads')), may hold values from 0 to 7, as said below
- attn_gain: float32 [2, 1024], replicated, may hold values from 0.5 to 1.5
- w_query: bfloat16 [2, 1024, 1024], P(None, None, 'heads'), may hold values from -0.1875 to 0.1875
- w_key: bfloat16 [2, 1024, 1024], P(None, None, 'heads'), may hold values from -0.1875 to 0.1875
- w_value: bfloat16 [2, 1024, 1024], P(None, None, 'heads'), may hold values from -0.1875 to 0.1875
- w_out: bfloat16 [2, 1024, 1024], P(None, 'heads'), may hold values from -0.75 to 0.75
- mlp_gain: float32 [2, 1024], replicated, may hold values from 0.5 to 1.5
- w_gate: bfloat16 [2, 1024, 2816], P(None, None, 'hid'), may hold values from -0.1875 to 0.1875
- w_up: bfloat16 [2, 1024, 2816], P(None, None, 'hid'), may hold values from -0.1875 to 0.1875
- w_down: bfloat16 [2, 2816, 1024], P(None, 'hid'), may hold values from -0.109375 to 0.109375
Outputs:
- block_out: bfloat16 [8192, 1024], P(('hid', 'heads'))
- input_grad: float32 [8192, 1024], P(('hid', 'heads'))
- attn_gain_grad: float32 [2, 1024], replicated
- query_grad: float32 [2, 1024, 1024], P(None, None, 'heads')
- key_grad: float32 [2, 1024, 1024], P(None, None, 'heads')
- value_grad: float32 [2, 1024, 1024], P(None, None, 'heads')
- out_grad: float32 [2, 1024, 1024], P(None, 'heads')
- mlp_gain_grad: float32 [2, 1024], replicated
- gate_grad: float32 [2, 1024, 2816], P(None, None, 'hid')
- up_grad: float32 [2, 1024, 2816], P(None, None, 'hid')
- down_grad: float32 [2, 2816, 1024], P(None, 'hid')
The draws below stay inside these ranges and needn't reach their ends.
Inputs may be any that keep to these rules, and one draw needn't show every extreme that they name: `segments`: segment numbers never fall along the tokens; group k of 2048 consecutive tokens uses numbers from k * (2) to (k + 1) * 2 - 1 and holds whole sequences whose lengths are multiples of 1024; in one group, drawn from the seed, all tokens form one sequence.
All inputs are finite; a program needn't handle non-finite values.
Results may differ from the reference program's by a relative error of at most 0.035.
Values may be sent and summed in bfloat16 or wider, within the bound.
No kernel may reach another device: no remote copies, remote signals or barrier semaphores. Data moves between devices by JAX's collectives and lax.ppermute only.
A program may use at most 256 MiB of HBM per device.

```python
import jax
import jax.numpy as jnp
from jax import lax

D = 1024
HEADS = 16
HEAD_DIM = 64
FF = 2816
LAYERS = 2
SEQ_UNIT = 1024
GROUP = 2048
GROUPS = 4
TOKENS = 8192


def draw_segments(key, part):
    key = jax.random.fold_in(key, 11)
    unit_count = GROUP // SEQ_UNIT
    unit_breaks = jax.random.randint(jax.random.fold_in(key, 1), (GROUPS, unit_count), 0, 2).astype(jnp.int32)
    not_first = (jnp.arange(unit_count, dtype=jnp.int32) > 0).astype(jnp.int32)
    whole_group = jax.random.randint(jax.random.fold_in(key, 2), (), 0, GROUPS).astype(jnp.int32)
    open_groups = (jnp.arange(GROUPS, dtype=jnp.int32) != whole_group).astype(jnp.int32)
    unit_breaks = unit_breaks * not_first[None, :] * open_groups[:, None]
    rising = jnp.cumsum(unit_breaks, axis=1).astype(jnp.int32)
    break_total = jnp.sum(unit_breaks, axis=1, keepdims=True).astype(jnp.int32)
    from_end = unit_count - 1 - break_total + rising
    first_group = (jnp.arange(GROUPS, dtype=jnp.int32) == 0)[:, None]
    segment_local = jnp.where(first_group, rising, from_end).astype(jnp.int32)
    segment_numbers = jnp.arange(GROUPS, dtype=jnp.int32)[:, None] * unit_count + segment_local
    return jnp.repeat(segment_numbers, SEQ_UNIT, axis=1).reshape(GROUPS * GROUP).astype(jnp.int32)


def levels(rng, dims, split, least, largest):
    loudness, own = 1.0, jax.random.fold_in(rng, 6)
    for position, blocks in split:
        draws = jnp.exp(jax.random.uniform(jax.random.fold_in(own, position), (blocks,), jnp.float32, least / len(split), largest / len(split)))
        loudness = loudness * jnp.repeat(draws, dims[position] // blocks).reshape([-1 if axis == position else 1 for axis in range(len(dims))])
    return loudness


def gaussian(stream_key, shape, scale, most, shards=(), kind=jnp.bfloat16):
    loudness = levels(stream_key, shape, shards, -0.22, 0.18) if shards else 1.0
    drawn = jax.random.normal(stream_key, shape, jnp.float32) * scale * loudness
    return jnp.minimum(jnp.maximum(drawn, -most), most).astype(kind)


def setup_inputs(seed: int = 0) -> dict:
    splits = jax.random.split(jax.random.key(seed), 13)
    inputs = gaussian(splits[0], (TOKENS, D), 1.0, 6.0, ((0, 32),))
    cotangent = gaussian(splits[1], (TOKENS, D), 1.0, 6.0, ((0, 32),))
    segments = draw_segments(jax.random.fold_in(splits[12], 71), 0)
    attn_gain = jnp.clip(1.0 + 0.1 * jax.random.normal(splits[3], (LAYERS, D), jnp.float32), 0.5, 1.5)
    w_query = gaussian(splits[4], (LAYERS, D, HEADS * HEAD_DIM), D ** -0.5, 0.1875, ((2, 8),))
    w_key = gaussian(splits[5], (LAYERS, D, HEADS * HEAD_DIM), D ** -0.5, 0.1875, ((2, 8),))
    w_value = gaussian(splits[6], (LAYERS, D, HEADS * HEAD_DIM), D ** -0.5, 0.1875, ((2, 8),))
    w_out = gaussian(splits[7], (LAYERS, HEADS * HEAD_DIM, D), (D // 16) ** -0.5, 0.75, ((1, 8),))
    mlp_gain = jnp.clip(1.0 + 0.1 * jax.random.normal(splits[8], (LAYERS, D), jnp.float32), 0.5, 1.5)
    w_gate = gaussian(splits[9], (LAYERS, D, FF), D ** -0.5, 0.1875, ((2, 4),))
    w_up = gaussian(splits[10], (LAYERS, D, FF), D ** -0.5, 0.1875, ((2, 4),))
    w_down = gaussian(splits[11], (LAYERS, FF, D), FF ** -0.5, 0.109375, ((1, 4),))
    return {"inputs": inputs, "cotangent": cotangent, "segments": segments, "attn_gain": attn_gain, "w_query": w_query, "w_key": w_key, "w_value": w_value, "w_out": w_out, "mlp_gain": mlp_gain, "w_gate": w_gate, "w_up": w_up, "w_down": w_down}


EPSILON = 1e-06
THETA = 10000.0
HIGH = lax.Precision.HIGHEST

@jax.custom_vjp
def low(v):
    return lax.optimization_barrier(v.astype(jnp.bfloat16)).astype(jnp.float32)

@jax.custom_vjp
def low_back(v):
    return v

def low_keep(v):
    return (low(v), None)

def low_pass(kept, grad):
    return (grad,)

def back_keep(v):
    return (v, None)

def back_low(kept, grad):
    return (low(grad),)
low.defvjp(low_keep, low_pass)
low_back.defvjp(back_keep, back_low)

def rms_scale(values, gain):
    return values * lax.rsqrt(lax.optimization_barrier(jnp.mean(values * values, axis=-1, keepdims=True)) + EPSILON) * gain

def positions_of(segment_row):
    row_count = segment_row.shape[0]
    row_index = jnp.arange(row_count, dtype=jnp.int32)
    changes = jnp.concatenate([jnp.ones((1,), dtype=jnp.bool_), segment_row[1:] != segment_row[:-1]])
    seq_starts = lax.cummax(jnp.where(changes, row_index, jnp.zeros_like(row_index)), axis=0)
    return row_index - seq_starts

def rope_tables(segment_row):
    positions = positions_of(segment_row).astype(jnp.float32)
    halfway = HEAD_DIM // 2
    frequency = THETA ** (-jnp.arange(halfway, dtype=jnp.float32) * 2.0 / HEAD_DIM)
    angles = positions[:, None] * frequency[None, :]
    return (jnp.cos(angles), jnp.sin(angles))

def rotate_pairs(flat, cosine, sine):
    shaped = flat.reshape(flat.shape[0], -1, HEAD_DIM)
    halfway = HEAD_DIM // 2
    former = shaped[..., :halfway]
    latter = shaped[..., halfway:]
    cos_rows = cosine[:, None, :]
    sin_rows = sine[:, None, :]
    turned = jnp.concatenate([former * cos_rows - latter * sin_rows, latter * cos_rows + former * sin_rows], axis=-1)
    return turned.reshape(flat.shape)

def attend_group(normed, segment_row, w_query, w_key, w_value, w_out, value_first):
    group_rows = normed.shape[0]
    block_rows = min(512, group_rows)
    cosine, sine = rope_tables(segment_row)
    queries = low(rotate_pairs(low_back(jnp.dot(normed, w_query, precision=HIGH)), cosine, sine))
    keys = low(rotate_pairs(low_back(jnp.dot(normed, w_key, precision=HIGH)), cosine, sine))
    value_raw = jnp.dot(normed, w_value, precision=HIGH)
    if value_first is None:
        values = low(low_back(value_raw))
    else:
        values = low(low_back(0.5 * value_raw + 0.5 * value_first))
    query_heads = queries.reshape(group_rows, HEADS, HEAD_DIM)
    key_heads = keys.reshape(group_rows, HEADS, HEAD_DIM)
    value_heads = values.reshape(group_rows, HEADS, HEAD_DIM)
    score_scale = HEAD_DIM ** (-0.5)

    def one_block(number):
        first_row = (number * block_rows).astype(jnp.int32)
        query_block = lax.dynamic_slice_in_dim(query_heads, first_row, block_rows, 0)
        query_segments = lax.dynamic_slice_in_dim(segment_row, first_row, block_rows, 0)
        query_index = first_row + jnp.arange(block_rows, dtype=jnp.int32)
        key_index = jnp.arange(group_rows, dtype=jnp.int32)
        allowed = (query_segments[:, None] == segment_row[None, :]) & (key_index[None, :] <= query_index[:, None])
        scores = low_back(jnp.einsum('qhe,khe->hqk', query_block, key_heads, precision=HIGH) * score_scale)
        scores = jnp.where(allowed[None], scores, -1e+30)
        highest = lax.optimization_barrier(jnp.max(scores, axis=-1, keepdims=True))
        exponent = jnp.exp(scores - highest)
        softmax_rows = exponent / lax.optimization_barrier(jnp.sum(exponent, axis=-1, keepdims=True))
        attended = jnp.einsum('hqk,khe->qhe', low(softmax_rows), value_heads, precision=HIGH)
        return low(low_back(attended))
    attended = lax.map(jax.checkpoint(one_block), jnp.arange(group_rows // block_rows, dtype=jnp.int32))
    attended = attended.reshape(group_rows, HEADS * HEAD_DIM)
    return (low_back(jnp.dot(attended, w_out, precision=HIGH)), values)

def feed_forward(normed, w_gate, w_up, w_down):
    gate = low_back(jnp.dot(normed, w_gate, precision=HIGH))
    upward = low_back(jnp.dot(normed, w_up, precision=HIGH))
    hidden = low(gate * jax.nn.sigmoid(gate) * upward)
    return low_back(jnp.dot(hidden, w_down, precision=HIGH))

def forward(inputs, attn_gain, w_query, w_key, w_value, w_out, mlp_gain, w_gate, w_up, w_down, segments):
    residual = inputs
    segment_groups = segments.reshape(GROUPS, GROUP)
    value_first = None
    for layer_index in range(LAYERS):
        normed = low(rms_scale(residual, attn_gain[layer_index]))
        normed_groups = normed.reshape(GROUPS, GROUP, D)
        query_layer = w_query[layer_index]
        key_layer = w_key[layer_index]
        value_layer = w_value[layer_index]
        out_layer = w_out[layer_index]
        if value_first is None:
            attn_groups, value_groups = lax.map(lambda pair: attend_group(pair[0], pair[1], query_layer, key_layer, value_layer, out_layer, None), (normed_groups, segment_groups))
            value_first = value_groups
        else:
            attn_groups, value_groups = lax.map(lambda triple: attend_group(triple[0], triple[1], query_layer, key_layer, value_layer, out_layer, triple[2]), (normed_groups, segment_groups, value_first))
        residual = residual + attn_groups.reshape(TOKENS, D)
        mixed = low(rms_scale(residual, mlp_gain[layer_index]))
        residual = residual + feed_forward(mixed, w_gate[layer_index], w_up[layer_index], w_down[layer_index])
    return residual

def reference(inputs, cotangent, segments, attn_gain, w_query, w_key, w_value, w_out, mlp_gain, w_gate, w_up, w_down):

    def wrapped(arg_inputs, arg_attn_gain, arg_query, arg_key, arg_value, arg_out, arg_mlp_gain, arg_gate, arg_up, arg_down):
        return forward(arg_inputs, arg_attn_gain, arg_query, arg_key, arg_value, arg_out, arg_mlp_gain, arg_gate, arg_up, arg_down, segments)
    result, pull_back = jax.vjp(wrapped, inputs.astype(jnp.float32), attn_gain.astype(jnp.float32), w_query.astype(jnp.float32), w_key.astype(jnp.float32), w_value.astype(jnp.float32), w_out.astype(jnp.float32), mlp_gain.astype(jnp.float32), w_gate.astype(jnp.float32), w_up.astype(jnp.float32), w_down.astype(jnp.float32))
    grads = pull_back(cotangent.astype(jnp.float32))
    return (result.astype(jnp.bfloat16), grads[0], grads[1], grads[2], grads[3], grads[4], grads[5], grads[6], grads[7], grads[8], grads[9])
```

```python
import functools

import jax
import jax.numpy as jnp
import numpy as np
from jax import lax
from jax.experimental import pallas as pl
from jax.experimental.pallas import tpu as pltpu
from jax.sharding import Mesh
from jax.sharding import PartitionSpec as P

HEAD_DIM = 64
SEQ_UNIT = 1024
EPSILON = 1e-06
THETA = 10000.0
NEG_LARGE = -1e30
BF16 = jnp.bfloat16
F32 = jnp.float32
VMEM_BYTES = 40 * 1024 * 1024

NT = (((1,), (1,)), ((), ()))
TN = (((0,), (0,)), ((), ()))


def swap(value, axes):
    axes = tuple(axes)
    size = 2 ** len(axes)
    return lax.ppermute(
        value, axes if len(axes) > 1 else axes[0], [(i, size - 1 - i) for i in range(size)]
    )


def axes_of(bits, axes):
    count = len(axes)
    return tuple(a for n, a in enumerate(axes) if bits >> (count - 1 - n) & 1)


def gather(value, axes, core):
    if len(axes) == 2:
        half = value.shape[-1] // 2
        low = swap(value, axes[1:])
        high = swap(value, axes[:1])
        both = jnp.concatenate(
            [swap(low[..., :half], axes[:1]), swap(high[..., half:], axes[1:])], axis=-1
        )
        chips = [value, low, high, both]
    else:
        chips = [value] + [swap(value, axes_of(i, axes)) for i in range(1, 2 ** len(axes))]
    return jnp.stack([jnp.stack(chips), jnp.stack([swap(c, (core,)) for c in chips])])


def scatter_sum(parts, axes, core):
    mine = parts[0].astype(F32) + swap(parts[1], (core,)).astype(F32)
    sent = mine.astype(BF16)
    total = mine[0]
    for i in range(1, 2 ** len(axes)):
        total = total + swap(sent[i], axes_of(i, axes)).astype(F32)
    return total


def heads_to_tokens(blocks, axes, core):
    other = swap(blocks[1], (core,))
    pairs = jnp.stack([blocks[0], other])
    chips = [pairs[:, 0]] + [
        swap(pairs[:, i], axes_of(i, axes)) for i in range(1, 2 ** len(axes))
    ]
    stacked = jnp.stack(chips, axis=1)
    count = stacked.shape[0] * stacked.shape[1]
    rows, width = stacked.shape[2:]
    return stacked.reshape(count, rows, width).transpose(1, 0, 2).reshape(rows, count * width)


def tokens_to_heads(rows_all, axes, core):
    chip_count = 2 ** len(axes)
    rows = rows_all.shape[0]
    width = rows_all.shape[1] // (2 * chip_count)
    blocks = rows_all.reshape(rows, 2, chip_count, width).transpose(1, 2, 0, 3)
    chips = [blocks[:, 0]] + [
        swap(blocks[:, i], axes_of(i, axes)) for i in range(1, chip_count)
    ]
    stacked = jnp.stack(chips, axis=1)
    return jnp.stack([stacked[0], swap(stacked[1], (core,))])


def exchange_sum(value, axes):
    for axis in axes:
        value = (value.astype(F32) + swap(value, (axis,)).astype(F32)).astype(BF16)
    return value


TURN = [(0, 0), (1, 2), (2, 1), (3, 3)]
CROSS = [(0, 1), (1, 3), (2, 0), (3, 2)]
CROSS_BACK = [(b, a) for a, b in CROSS]


def compiler_params():
    return pltpu.CompilerParams(vmem_limit_bytes=VMEM_BYTES)


VMEM = functools.partial(pl.BlockSpec, memory_space=pltpu.VMEM)
SMEM = functools.partial(pl.BlockSpec, memory_space=pltpu.SMEM)


def half_turn(value):
    width = value.shape[-1]
    halfway = HEAD_DIM // 2
    if width == HEAD_DIM:
        return jnp.concatenate([value[:, halfway:], value[:, :halfway]], axis=-1)
    lane = lax.broadcasted_iota(jnp.int32, value.shape, 1)
    return jnp.where(
        lane % HEAD_DIM < halfway,
        pltpu.roll(value, width - halfway, 1),
        pltpu.roll(value, halfway, 1),
    )


def head_masked(value, head):
    if value.shape[-1] == HEAD_DIM:
        return value
    lane = lax.broadcasted_iota(jnp.int32, value.shape, 1)
    return jnp.where(lane // HEAD_DIM == head, value, jnp.zeros_like(value))


def project_kernel(mixed, chips, rows, width, *refs):
    ids, normed, weights, cosine, sine = refs[:5]
    first = refs[5] if mixed else None
    queries, keys, values = refs[-3:]
    for core in range(2):
        block = normed[core].reshape(chips * rows, normed.shape[-1])
        raw = jnp.dot(block, weights[...], preferred_element_type=F32)
        for chip in range(chips):
            place = (chip ^ ids[0]) * 2 + (core ^ ids[1])
            at = pl.ds(pl.multiple_of(place * rows, rows), rows)
            piece = raw[chip * rows : (chip + 1) * rows]
            query, key, value = (piece[:, n * width : (n + 1) * width] for n in range(3))
            cos, sin = cosine[at, :], sine[at, :]
            queries[at, :] = ((query * cos + half_turn(query) * sin) * HEAD_DIM**-0.5).astype(BF16)
            keys[at, :] = (key * cos + half_turn(key) * sin).astype(BF16)
            if mixed:
                value = 0.5 * value + 0.5 * first[at, :].astype(F32)
            values[at, :] = value.astype(BF16)


def project(ids, normed, weights, cosine, sine, first):
    _, chips, rows, depth = normed.shape
    width = weights.shape[1] // 3
    count = 2 * chips * rows
    out = jax.ShapeDtypeStruct((count, width), BF16)
    operands = (ids, normed, weights, cosine, sine) + (() if first is None else (first,))
    return pl.pallas_call(
        functools.partial(project_kernel, first is not None, chips, rows, width),
        out_shape=(out, out, out),
        in_specs=[SMEM()] + [VMEM()] * (len(operands) - 1),
        out_specs=(VMEM(),) * 3,
        compiler_params=compiler_params(),
        cost_estimate=pl.CostEstimate(
            flops=2 * count * depth * 3 * width,
            bytes_accessed=2 * count * depth + 6 * depth * width + 14 * count * width,
            transcendentals=0,
        ),
        name="project_heads",
    )(*operands)


def attend_kernel(number, unit_count, chips, rows, width, *refs):
    ids = refs[0]
    queries = refs[1]
    key_refs = refs[2 : 3 + number]
    value_refs = refs[3 + number : 4 + 2 * number]
    attended, log_totals = refs[-2:]
    heads = width // HEAD_DIM
    block = 2 * rows
    count = chips * block
    units = max(count // SEQ_UNIT, 1)
    unit_rows = count // units

    def allowed(query_unit, key_unit):
        return ids[2 + query_unit * unit_count + key_unit] > 0

    for chip in range(chips):
        first = chip * block
        own_unit = number * units + first // unit_rows
        segments = []
        for part in range(number):
            for unit in range(units):
                segments.append((part, unit * unit_rows, unit_rows, part * units + unit, False))
        for unit in range(first // unit_rows):
            segments.append((number, unit * unit_rows, unit_rows, number * units + unit, False))
        unit_start = first // unit_rows * unit_rows
        if first > unit_start:
            segments.append((number, unit_start, first - unit_start, None, False))
        segments.append((number, first, block, None, True))
        query_all = queries[first : first + block, :]
        outs = None
        lane = lax.broadcasted_iota(jnp.int32, (block, 128), 1)
        totals_wide = jnp.zeros((block, 128), F32)
        for head in range(heads):
            query = head_masked(query_all, head)
            scores, biases, tops = [], [], []
            for part, start, length, unit, diagonal in segments:
                score = lax.dot_general(
                    query, key_refs[part][start : start + length, :], NT,
                    preferred_element_type=F32,
                )
                if diagonal:
                    row = lax.broadcasted_iota(jnp.int32, score.shape, 0)
                    column = lax.broadcasted_iota(jnp.int32, score.shape, 1)
                    score = jnp.where(column <= row, score, NEG_LARGE)
                bias = 0.0 if unit is None else jnp.where(allowed(own_unit, unit), 0.0, NEG_LARGE)
                scores.append(score)
                biases.append(bias)
                tops.append(jnp.max(score, axis=1, keepdims=True) + bias)
            highest = functools.reduce(jnp.maximum, tops)
            summed, total = None, None
            for (part, start, length, unit, diagonal), score, bias in zip(segments, scores, biases):
                weight = jnp.exp(score - (highest - bias))
                narrow = weight.astype(BF16)
                value = value_refs[part][start : start + length, :]
                if heads > 1:
                    value_lane = lax.broadcasted_iota(jnp.int32, value.shape, 1)
                    value = jnp.where(value_lane // HEAD_DIM == head, value, jnp.ones_like(value))
                else:
                    part_total = jnp.sum(weight, axis=1, keepdims=True)
                    total = part_total if total is None else total + part_total
                product = jnp.dot(narrow, value, preferred_element_type=F32)
                summed = product if summed is None else summed + product
            if heads > 1:
                spread = pltpu.roll(summed, HEAD_DIM, 1)
                divided = head_masked(summed / spread, head)
                other = 1 - head
                total = spread if head == 0 else spread
                total = jnp.where(lane // HEAD_DIM == head, total, summed)
                logs = highest + jnp.log(total)
            else:
                divided = summed / total
                logs = jnp.broadcast_to(highest + jnp.log(total), (block, 128))
            outs = divided if outs is None else outs + divided
            totals_wide = jnp.where(lane == head, logs, totals_wide)
        rounded = outs.astype(BF16)
        place = chip ^ ids[0]
        for core in range(2):
            attended[core ^ ids[1], place] = rounded[core * rows : (core + 1) * rows]
        log_totals[:, first : first + block] = totals_wide.T[:8]


def attend(ids, unit_count, queries, keys, values, chips, rows):
    number = len(keys) - 1
    count, width = queries.shape
    heads = width // HEAD_DIM
    pairs = count * count // 2 + number * count * count
    return pl.pallas_call(
        functools.partial(attend_kernel, number, unit_count, chips, rows, width),
        out_shape=(
            jax.ShapeDtypeStruct((2, chips, rows, width), BF16),
            jax.ShapeDtypeStruct((8, count), F32),
        ),
        in_specs=[SMEM()] + [VMEM()] * (3 + 2 * number),
        out_specs=(VMEM(),) * 2,
        compiler_params=compiler_params(),
        cost_estimate=pl.CostEstimate(
            flops=heads * pairs * 256 * 4,
            bytes_accessed=2 * count * width * (4 + 2 * number),
            transcendentals=heads * pairs,
        ),
        name="attend_forward",
    )(ids, queries, *keys, *values)


def attend_back_kernel(number, last, unit_count, chips, rows, width, layer_first, *refs):
    refs = list(refs)
    ids = refs.pop(0)
    queries = refs.pop(0)
    key_refs = [refs.pop(0) for _ in range(number + 1)]
    value_refs = [refs.pop(0) for _ in range(number + 1)]
    attended, grads, log_totals, cosine, sine = (refs.pop(0) for _ in range(5))
    later_keys, later_values = (None, None) if last else (refs.pop(0), refs.pop(0))
    later_layer = refs.pop(0) if layer_first else None
    outs = refs.pop(0)
    earlier = [(refs.pop(0), refs.pop(0)) for _ in range(number)]
    grad_rows, inner, query_total, key_total, value_total = refs
    heads = width // HEAD_DIM
    block = 2 * rows
    count = chips * block
    units = max(count // SEQ_UNIT, 1)
    unit_rows = count // units

    def allowed(query_unit, key_unit):
        return ids[2 + query_unit * unit_count + key_unit] > 0

    def place_of(core, chip):
        place = (chip ^ ids[0]) * 2 + (core ^ ids[1])
        return pl.ds(pl.multiple_of(place * rows, rows), rows)

    for core in range(2):
        for chip in range(chips):
            at = place_of(core, chip)
            grad = grads[core, chip]
            grad_rows[at, :] = grad
            query_total[at, :] = grad.astype(F32) * attended[core, chip].astype(F32)
    turned = query_total[...].T
    for head in range(heads):
        inner[head : head + 1, :] = jnp.sum(
            turned[head * HEAD_DIM : (head + 1) * HEAD_DIM], axis=0, keepdims=True
        )
    query_total[...] = jnp.zeros_like(query_total)
    if last:
        key_total[...] = jnp.zeros_like(key_total)
        value_total[...] = jnp.zeros_like(value_total)
    else:
        key_total[...] = later_keys[...]
        value_total[...] = later_values[...]
    for key_out, value_out in earlier:
        key_out[...] = jnp.zeros_like(key_out)
        value_out[...] = jnp.zeros_like(value_out)

    def work(part, key_start, key_count, query_start, diagonal):
        keys, values = key_refs[part], value_refs[part]
        key_sum, value_sum = (key_total, value_total) if part == number else earlier[part]
        at = pl.ds(key_start, key_count)
        query_at = pl.ds(query_start, block)
        key, value = keys[at, :], values[at, :]
        key_part, value_part, query_part = None, None, None
        for head in range(heads):
            query = head_masked(queries[query_at, :], head)
            grad = head_masked(grad_rows[query_at, :], head)
            score = lax.dot_general(key, query, NT, preferred_element_type=F32)
            weight = jnp.exp(score - log_totals[head : head + 1, query_at])
            if diagonal:
                row = lax.broadcasted_iota(jnp.int32, score.shape, 0)
                column = lax.broadcasted_iota(jnp.int32, score.shape, 1)
                weight = jnp.where(row + (key_start - query_start) <= column, weight, 0.0)
            back = lax.dot_general(value, grad, NT, preferred_element_type=F32)
            score_back = (weight * (back - inner[head : head + 1, query_at])).astype(BF16)
            narrow = weight.astype(BF16)
            value_term = jnp.dot(narrow, grad, preferred_element_type=F32)
            key_term = jnp.dot(score_back, query, preferred_element_type=F32)
            query_term = lax.dot_general(
                score_back, head_masked(key, head), TN, preferred_element_type=F32
            )
            if head == 0:
                key_part, value_part, query_part = key_term, value_term, query_term
            else:
                key_part, value_part, query_part = (
                    key_part + key_term, value_part + value_term, query_part + query_term,
                )
        key_sum[at, :] += key_part
        value_sum[at, :] += value_part
        query_total[query_at, :] += query_part

    for unit in range(units):
        start = unit * unit_rows
        blocks = unit_rows // block
        own_unit = number * units + unit
        others = [(part, other) for part in range(number) for other in range(units)]
        others += [(number, other) for other in range(unit)]
        for part, other in others:
            @pl.when(allowed(own_unit, part * units + other))
            def _():
                @pl.loop(0, blocks)
                def _(index):
                    work(part, other * unit_rows, unit_rows, start + index * block, False)
        for index in range(blocks):
            if index:
                work(number, start, index * block, start + index * block, False)
            work(number, start + index * block, block, start + index * block, True)

    for core in range(2):
        for chip in range(chips):
            at = place_of(core, chip)
            cos, sin = cosine[at, :], sine[at, :]
            query = query_total[at, :] * HEAD_DIM**-0.5
            key = key_total[at, :]
            value = value_total[at, :]
            query = query * cos - half_turn(query) * sin
            key = key * cos - half_turn(key) * sin
            if layer_first:
                value = value + later_layer[core, chip, :, 2 * width :].astype(F32)
            else:
                value = value.astype(BF16).astype(F32) * 0.5
            outs[core, chip] = jnp.concatenate([query, key, value], axis=1).astype(BF16)


def attend_back(
    ids, unit_count, queries, keys, values, attended, grads, log_totals, cosine, sine, later,
    later_layer,
):
    number = len(keys) - 1
    last = later is None
    _, chips, rows, width = attended.shape
    count = queries.shape[0]
    heads = width // HEAD_DIM
    pairs = count * count // 2 + number * count * count
    operands = [ids, queries, *keys, *values, attended, grads, log_totals, cosine, sine]
    if not last:
        operands += list(later)
    if later_layer is not None:
        operands.append(later_layer)
    total = jax.ShapeDtypeStruct((count, width), F32)
    return pl.pallas_call(
        functools.partial(
            attend_back_kernel, number, last, unit_count, chips, rows, width,
            later_layer is not None,
        ),
        out_shape=(jax.ShapeDtypeStruct((2, chips, rows, 3 * width), BF16),)
        + (total,) * (2 * number),
        in_specs=[SMEM()] + [VMEM()] * (len(operands) - 1),
        out_specs=(VMEM(),) * (1 + 2 * number),
        scratch_shapes=[
            pltpu.VMEM((count, width), BF16),
            pltpu.VMEM((8, count), F32),
            pltpu.VMEM((count, width), F32),
            pltpu.VMEM((count, width), F32),
            pltpu.VMEM((count, width), F32),
        ],
        compiler_params=compiler_params(),
        cost_estimate=pl.CostEstimate(
            flops=heads * pairs * 256 * 10,
            bytes_accessed=2 * count * width * 20,
            transcendentals=heads * pairs,
        ),
        name="attend_backward",
    )(*operands)


def rms_factor(values):
    return lax.rsqrt(jnp.mean(values * values, axis=-1, keepdims=True) + EPSILON)


def normed_rows(values, gain):
    return (values * rms_factor(values) * gain).astype(BF16)


def norm_back(values, gain, back):
    factor = rms_factor(values)
    scaled = back * gain
    mean = jnp.mean(scaled * values, axis=-1, keepdims=True)
    gain_grad = jnp.sum(back * values * factor, axis=0)
    return factor * scaled - values * (factor * factor * factor * mean), gain_grad


def matmul(left, right):
    return jnp.dot(left, right, preferred_element_type=F32)


def matmul_nt(left, right):
    return lax.dot_general(left, right, NT, preferred_element_type=F32)


def matmul_tn(left, right):
    return lax.dot_general(left, right, TN, preferred_element_type=F32)


def flat(blocks):
    return blocks.reshape(-1, blocks.shape[-1])


def per_device(
    head_axes, hid_axes, inputs, cotangent, segments, attn_gain, w_query, w_key, w_value, w_out,
    mlp_gain, w_gate, w_up, w_down,
):
    layers = w_query.shape[0]
    core = hid_axes[-1]
    group_axes = head_axes[1:]
    share_axes = hid_axes[:-1]
    chips = 2 ** len(group_axes)
    token_count = inputs.shape[0]
    rows = token_count // 2
    count = chips * token_count
    width = w_query.shape[2]
    units = max(count // SEQ_UNIT, 1)
    unit_count = 2 * units
    turn_axes = (head_axes[0], core)
    top = lax.axis_index(head_axes[0])
    core_at = lax.axis_index(core)
    chip_at = jnp.int32(0)
    for axis in group_axes:
        chip_at = chip_at * 2 + lax.axis_index(axis)

    def turn(value):
        return lax.ppermute(value, turn_axes, TURN)

    def take(value):
        own = lax.dynamic_slice_in_dim(value, top * rows, rows, 0)
        cross = lax.dynamic_slice_in_dim(value, (1 - top) * rows, rows, 0)
        own = lax.ppermute(own, turn_axes, TURN)
        cross = lax.ppermute(cross, turn_axes, CROSS)
        return [jnp.where(core_at == 0, own, cross), jnp.where(core_at == 0, cross, own)]

    def give(values):
        own = jnp.where(core_at == 0, values[0], values[1])
        cross = jnp.where(core_at == 0, values[1], values[0])
        own = lax.ppermute(own, turn_axes, TURN)
        cross = lax.ppermute(cross, turn_axes, CROSS_BACK)
        return jnp.where(
            top == 0,
            jnp.concatenate([own, cross], axis=0),
            jnp.concatenate([cross, own], axis=0),
        )

    number = turn(jnp.broadcast_to(segments[:1], (8, 128)))
    unit_axes = group_axes[: (units - 1).bit_length()]
    numbers = jnp.stack(
        [number] + [swap(number, axes_of(i, unit_axes)) for i in range(1, units)]
    )
    numbers = jnp.stack([numbers, swap(numbers, (core,))])[:, :, 0, 0]
    unit_at = chip_at // (chips // units)
    numbers = jnp.stack(
        [
            lax.dynamic_slice(numbers, (half ^ core_at, unit ^ unit_at), (1, 1))[0, 0]
            for half in range(2)
            for unit in range(units)
        ]
    )
    same = (numbers[:, None] == numbers[None, :]).astype(jnp.int32)
    ids = jnp.concatenate([jnp.stack([chip_at, core_at]).astype(jnp.int32), same.reshape(-1)])
    earlier_units = np.tril(np.ones((unit_count, unit_count), np.int32), -1)
    starts = jnp.sum(same * earlier_units, axis=1) * SEQ_UNIT
    frequency = np.float32(THETA) ** (-np.arange(HEAD_DIM // 2, dtype=np.float32) * 2 / HEAD_DIM)
    frequency = np.tile(frequency.astype(np.float32), 2 * width // HEAD_DIM)[None]
    signs = np.where(np.arange(width) % HEAD_DIM < HEAD_DIM // 2, -1.0, 1.0).astype(np.float32)
    within = np.arange(count, dtype=np.int32) % SEQ_UNIT
    cosines, sines = [], []
    for half in range(2):
        offset = jnp.repeat(starts[half * units : (half + 1) * units], count // units)
        angles = (offset + within).astype(F32)[:, None] * frequency
        cosines.append(jnp.cos(angles))
        sines.append(jnp.sin(angles) * signs)

    residual = [part.astype(F32) for part in take(inputs)]
    w_heads = [
        turn(jnp.concatenate([w_query[n], w_key[n], w_value[n]], axis=1)) for n in range(layers)
    ]
    w_out_all = [flat(gather(turn(w_out[n]), group_axes, core)) for n in range(layers)]

    stored = []
    first_values = [None, None]
    for layer in range(layers):
        kept = []
        keys, values = [], []
        for half in range(2):
            before = residual[half]
            gathered = gather(normed_rows(before, attn_gain[layer]), group_axes, core)
            queries, key, value = project(
                ids, gathered, w_heads[layer], cosines[half], sines[half], first_values[half]
            )
            keys.append(key)
            values.append(value)
            attended, log_totals = attend(
                ids, unit_count, queries, list(keys), list(values), chips, rows
            )
            attended_rows = heads_to_tokens(attended, group_axes, core)
            middle = before + matmul(attended_rows, w_out_all[layer])
            mixed = flat(gather(normed_rows(middle, mlp_gain[layer]), share_axes, core))
            gate = matmul(mixed, w_gate[layer])
            upward = matmul(mixed, w_up[layer])
            hidden = (gate * jax.nn.sigmoid(gate) * upward).astype(BF16)
            term = matmul(hidden, w_down[layer]).astype(BF16)
            term = term.reshape(2, -1, rows, term.shape[-1])
            residual[half] = middle + scatter_sum(term, share_axes, core)
            kept.append(
                dict(
                    before=before, gathered=gathered, queries=queries, attended=attended,
                    log_totals=log_totals, attended_rows=attended_rows, middle=middle, mixed=mixed,
                )
            )
        if layer == 0:
            first_values = values
        stored.append((kept, keys, values))
    block_out = give([part.astype(BF16) for part in residual])

    grad = [part.astype(F32) for part in take(cotangent)]
    attn_grads, out_grads, mlp_grads = [], [], []
    attn_gain_grads, mlp_gain_grads = [], []
    later_layer = [None, None]
    for layer in reversed(range(layers)):
        kept, keys, values = stored[layer]
        later = None
        sums = [None] * 7
        this_layer = [None, None]

        def accumulate(index, term):
            sums[index] = term if sums[index] is None else sums[index] + term

        for half in (1, 0):
            k = kept[half]
            down_in = flat(gather(grad[half].astype(BF16), share_axes, core))
            mixed = k["mixed"]
            gate = matmul(mixed, w_gate[layer])
            upward = matmul(mixed, w_up[layer])
            sigmoid = jax.nn.sigmoid(gate)
            hidden = (gate * sigmoid * upward).astype(BF16)
            hidden_grad = matmul_nt(down_in, w_down[layer])
            gate_back = (hidden_grad * upward * sigmoid * (1 + gate * (1 - sigmoid))).astype(BF16)
            up_back = (hidden_grad * gate * sigmoid).astype(BF16)
            term = (matmul_nt(gate_back, w_gate[layer]) + matmul_nt(up_back, w_up[layer])).astype(
                BF16
            )
            normed_back = scatter_sum(
                term.reshape(2, -1, rows, term.shape[-1]), share_axes, core
            )
            part, gain_part = norm_back(k["middle"], mlp_gain[layer], normed_back)
            accumulate(0, gain_part)
            middle_back = grad[half] + part
            attn_in = middle_back.astype(BF16)
            back_rows = matmul_nt(attn_in, w_out_all[layer]).astype(BF16)
            attended_back = tokens_to_heads(back_rows, group_axes, core)
            results = attend_back(
                ids, unit_count, k["queries"], keys[: half + 1], values[: half + 1],
                k["attended"], attended_back, k["log_totals"], cosines[half], sines[half],
                later, later_layer[half],
            )
            raws = results[0]
            later = results[1:]
            this_layer[half] = raws
            term = matmul_nt(flat(raws), w_heads[layer]).astype(BF16)
            normed_in = scatter_sum(
                term.reshape(2, chips, rows, term.shape[-1]), group_axes, core
            )
            part, gain_part = norm_back(k["before"], attn_gain[layer], normed_in)
            accumulate(1, gain_part)
            grad[half] = middle_back + part
            accumulate(2, matmul_tn(hidden, down_in))
            accumulate(3, matmul_tn(mixed, gate_back))
            accumulate(4, matmul_tn(mixed, up_back))
            accumulate(5, matmul_tn(k["attended_rows"], attn_in))
            accumulate(6, matmul_tn(flat(k["gathered"]), flat(raws)))
        later_layer = this_layer
        mlp_gain_grads.append(sums[0])
        attn_gain_grads.append(sums[1])
        mlp_grads.append(
            [lax.psum(part.astype(BF16), head_axes).astype(F32) for part in sums[2:5]]
        )
        out_grad = scatter_sum(
            sums[5].astype(BF16).reshape(2, chips, width, -1), group_axes, core
        )
        back_axes = (core,) + share_axes
        out_grads.append(exchange_sum(turn(out_grad.astype(BF16)), back_axes).astype(F32))
        attn_grads.append(exchange_sum(turn(sums[6].astype(BF16)), back_axes).astype(F32))

    input_grad = give([part.astype(BF16) for part in grad]).astype(F32)
    gains = lax.psum(
        jnp.stack(attn_gain_grads[::-1] + mlp_gain_grads[::-1]), head_axes + hid_axes
    )

    def stacked(parts):
        return jnp.stack(parts[::-1])

    return (
        block_out,
        input_grad,
        gains[:layers],
        stacked([part[:, :width] for part in attn_grads]),
        stacked([part[:, width : 2 * width] for part in attn_grads]),
        stacked([part[:, 2 * width :] for part in attn_grads]),
        stacked(out_grads),
        gains[layers:],
        stacked([part[1] for part in mlp_grads]),
        stacked([part[2] for part in mlp_grads]),
        stacked([part[0] for part in mlp_grads]),
    )


def solution(mesh):
    head_bits = (mesh.shape["heads"] - 1).bit_length()
    hid_bits = (mesh.shape["hid"] - 1).bit_length()
    head_axes = tuple(f"heads{n}" for n in range(head_bits))
    hid_axes = tuple(f"hid{n}" for n in range(hid_bits))
    binary = Mesh(mesh.devices.reshape((2,) * (head_bits + hid_bits)), head_axes + hid_axes)
    tokens = hid_axes + head_axes
    in_specs = (
        P(tokens, None),
        P(tokens, None),
        P(tokens),
        P(),
        P(None, None, head_axes),
        P(None, None, head_axes),
        P(None, None, head_axes),
        P(None, head_axes, None),
        P(),
        P(None, None, hid_axes),
        P(None, None, hid_axes),
        P(None, hid_axes, None),
    )
    out_specs = (
        P(tokens, None),
        P(tokens, None),
        P(),
        P(None, None, head_axes),
        P(None, None, head_axes),
        P(None, None, head_axes),
        P(None, head_axes, None),
        P(),
        P(None, None, hid_axes),
        P(None, None, hid_axes),
        P(None, hid_axes, None),
    )
    return jax.shard_map(
        functools.partial(per_device, head_axes, hid_axes),
        mesh=binary,
        in_specs=in_specs,
        out_specs=out_specs,
        check_vma=False,
    )
```

```python
import functools

import jax
import jax.numpy as jnp
import numpy as np
from jax import lax
from jax.experimental import pallas as pl
from jax.experimental.pallas import tpu as pltpu
from jax.sharding import Mesh
from jax.sharding import PartitionSpec as P

HEAD_DIM = 64
SEQ_UNIT = 1024
EPSILON = 1e-06
THETA = 10000.0
NEG_LARGE = -1e30
BF16 = jnp.bfloat16
F32 = jnp.float32
VMEM_BYTES = 36 * 1024 * 1024
COST_SCALE = 50

NT = (((1,), (1,)), ((), ()))
TN = (((0,), (0,)), ((), ()))


def swap(value, axes):
    axes = tuple(sorted(axes))
    size = 2 ** len(axes)
    return lax.ppermute(
        value, axes if len(axes) > 1 else axes[0], [(i, size - 1 - i) for i in range(size)]
    )


def axes_of(bits, axes):
    count = len(axes)
    return tuple(a for n, a in enumerate(axes) if bits >> (count - 1 - n) & 1)


def gather_chips(value, axes):
    return [value] + [swap(value, axes_of(i, axes)) for i in range(1, 2 ** len(axes))]


def after(value, *others):
    return lax.optimization_barrier((value, *others))[0]


def gather(value, axes, core, *ties):
    if len(axes) == 2:
        half = value.shape[-1] // 2
        own = swap(value, (core,))
        low = swap(value, axes[1:])
        high = swap(value, axes[:1])
        low, high, own, *_ = lax.optimization_barrier((low, high, own, *ties))
        both = jnp.concatenate(
            [swap(low[..., :half], axes[:1]), swap(high[..., half:], axes[1:])], axis=-1
        )
        chips = [value, low, high, both]
        return chips, [own] + [swap(c, (core,)) for c in chips[1:]]
    chips = gather_chips(value, axes)
    return chips, [swap(c, (core,)) for c in chips]


def reduce_blocks(kept, received, axes):
    for axis in axes:
        if axis != axes[0]:
            received = swap(sent, (axis,))
        total = (kept.astype(F32) + received.astype(F32)).astype(BF16)
        half = total.shape[0] // 2
        kept, sent = total[:half], total[half:]
    return total


def spread_blocks(block, axes):
    for axis in reversed(axes):
        block = jnp.concatenate([block, swap(block, (axis,))], axis=0)
    return block


def scatter_sum(mine, others, axes, core, *ties):
    mine = mine + swap(others, (core,)).astype(F32)
    sent = after(mine.astype(BF16), *ties)
    total = mine[0]
    for i in range(1, 2 ** len(axes)):
        total = total + swap(sent[i], axes_of(i, axes)).astype(F32)
    return total


def exchange(blocks, axes, core):
    got = [blocks[0]] + [swap(blocks[i], axes_of(i, axes)) for i in range(1, 2 ** len(axes))]
    return got, swap(jnp.stack([g[1] for g in got]), (core,))


def exchange_sum(value, axes, kind=BF16):
    for axis in axes:
        value = (value.astype(F32) + swap(value, (axis,)).astype(F32)).astype(kind)
    return value


TURN = [(0, 0), (1, 2), (2, 1), (3, 3)]


def compiler_params():
    return pltpu.CompilerParams(vmem_limit_bytes=VMEM_BYTES)


def cost(flops, bytes_accessed, transcendentals):
    return pl.CostEstimate(
        flops=flops // COST_SCALE,
        bytes_accessed=bytes_accessed // COST_SCALE,
        transcendentals=transcendentals // COST_SCALE,
    )


VMEM = functools.partial(pl.BlockSpec, memory_space=pltpu.VMEM)
SMEM = functools.partial(pl.BlockSpec, memory_space=pltpu.SMEM)


def half_turn(value):
    width = value.shape[-1]
    halfway = HEAD_DIM // 2
    if width == HEAD_DIM:
        return jnp.concatenate([value[:, halfway:], value[:, :halfway]], axis=-1)
    lane = lax.broadcasted_iota(jnp.int32, value.shape, 1)
    return jnp.where(
        lane % HEAD_DIM < halfway,
        pltpu.roll(value, width - halfway, 1),
        pltpu.roll(value, halfway, 1),
    )


def head_masked(value, head):
    if value.shape[-1] == HEAD_DIM:
        return value
    lane = lax.broadcasted_iota(jnp.int32, value.shape, 1)
    return jnp.where(lane // HEAD_DIM == head, value, jnp.zeros_like(value))


def place_of(ids, core, chip, chips, rows):
    place = (core ^ ids[1]) * chips + (chip ^ ids[0])
    return pl.ds(pl.multiple_of(place * rows, rows), rows)


def pack_kernel(width, places, *refs):
    out = refs[-1]
    layers = out.shape[0]
    for layer in range(layers):
        for half in range(2):
            @pl.when(places[0] == half)
            def _():
                for n in range(2):
                    part = refs[2 * half + n][layer]
                    out[layer, n * width : (n + 1) * width] = part if half and n else part.T


def pack_heads(places, weights):
    layers, depth, width = weights[0].shape
    return pl.pallas_call(
        functools.partial(pack_kernel, width),
        out_shape=jax.ShapeDtypeStruct((layers, 2 * width, depth), BF16),
        in_specs=[SMEM()] + [VMEM()] * 4,
        out_specs=VMEM(),
        compiler_params=compiler_params(),
        cost_estimate=cost(
            flops=0, bytes_accessed=12 * layers * width * depth, transcendentals=0
        ),
        name="pack_head_weights",
    )(places, *weights)


def table_rows(ids, core, chip, chips, rows):
    count = 2 * chips * rows
    units = max(count // SEQ_UNIT, 1)
    first = ((core ^ ids[1]) * chips + (chip ^ ids[0])) * rows
    unit = first // (count // units)
    start = ids[2 + units * units + unit]
    return pl.ds(pl.multiple_of(start + first % (count // units), rows), rows)


def project_kernel(mixed, chips, rows, width, *refs):
    refs = list(refs)
    ids = refs.pop(0)
    blocks = [refs.pop(0) for _ in range(2 * chips)]
    weights, cosine, sine = (refs.pop(0) for _ in range(3))
    first = refs.pop(0) if mixed else None
    queries, keys, values = refs
    for number, block in enumerate(blocks):
        raw = lax.dot_general(block[...], weights[: 3 * width, :], NT, preferred_element_type=F32)
        at = place_of(ids, number // chips, number % chips, chips, rows)
        query, key, value = (raw[:, n * width : (n + 1) * width] for n in range(3))
        turn_at = table_rows(ids, number // chips, number % chips, chips, rows)
        cos, sin = cosine[turn_at, :], sine[turn_at, :]
        queries[at, :] = ((query * cos + half_turn(query) * sin) * HEAD_DIM**-0.5).astype(BF16)
        keys[at, :] = (key * cos + half_turn(key) * sin).astype(BF16)
        if mixed:
            value = 0.5 * value + 0.5 * first[at, :].astype(F32)
        values[at, :] = value.astype(BF16)


def project(ids, blocks, weights, cosine, sine, first):
    chips = len(blocks) // 2
    rows, depth = blocks[0].shape
    width = weights.shape[0] // 4
    count = 2 * chips * rows
    out = jax.ShapeDtypeStruct((count, width), BF16)
    operands = (ids, *blocks, weights, cosine, sine) + (() if first is None else (first,))
    return pl.pallas_call(
        functools.partial(project_kernel, first is not None, chips, rows, width),
        out_shape=(out, out, out),
        in_specs=[SMEM()] + [VMEM()] * (len(operands) - 1),
        out_specs=(VMEM(),) * 3,
        compiler_params=compiler_params(),
        cost_estimate=cost(
            flops=2 * count * depth * 3 * width,
            bytes_accessed=2 * count * depth + 6 * depth * width + 14 * count * width,
            transcendentals=0,
        ),
        name="project_heads",
    )(*operands)


def lanes_joined(pieces):
    return jnp.concatenate(pieces, axis=1)


def middle_kernel(chips, *refs):
    refs = list(refs)
    near = [refs.pop(0) for _ in range(chips)]
    far, weights, before, gain, attended_rows, middle, normed = refs
    rows = lanes_joined([n[0] for n in near] + [far[i] for i in range(chips)])
    attended_rows[...] = rows
    value = before[...] + jnp.dot(rows, weights[...], preferred_element_type=F32)
    middle[...] = value
    normed[...] = normed_rows(value, gain[...])


def middle_step(near, far, weights, before, gain):
    chips = len(near)
    rows, depth = before.shape
    features = weights.shape[0]
    return pl.pallas_call(
        functools.partial(middle_kernel, chips),
        out_shape=(
            jax.ShapeDtypeStruct((rows, features), BF16),
            jax.ShapeDtypeStruct((rows, depth), F32),
            jax.ShapeDtypeStruct((rows, depth), BF16),
        ),
        in_specs=[VMEM()] * (chips + 4),
        out_specs=(VMEM(),) * 3,
        compiler_params=compiler_params(),
        cost_estimate=cost(
            flops=2 * rows * features * depth,
            bytes_accessed=2 * features * depth + 14 * rows * depth,
            transcendentals=0,
        ),
        name="attention_out",
    )(*near, far, weights, before, gain)


def middle_back_kernel(chips, width, *refs):
    refs = list(refs)
    kept = refs.pop(0)
    middle, gain, weights, grad = refs[-8:-4]
    received = refs[:-8]
    total, rounded, gain_part, blocks = refs[-4:]
    back = kept[...]
    for term in received:
        back = back + term[...].astype(F32)
    part, gains = norm_back(middle[...], gain[...], back)
    value = grad[...] + part
    total[...] = value
    narrow = value.astype(BF16)
    rounded[...] = narrow
    gain_part[...] = jnp.broadcast_to(gains, gain_part.shape)
    heads = lax.dot_general(narrow, weights[...], NT, preferred_element_type=F32).astype(BF16)
    for core in range(2):
        for chip in range(chips):
            at = (core * chips + chip) * width
            blocks[chip, core] = heads[:, at : at + width]


def middle_back_step(kept, received, middle, gain, weights, grad, chips):
    rows, depth = middle.shape
    width = weights.shape[0] // (2 * chips)
    return pl.pallas_call(
        functools.partial(middle_back_kernel, chips, width),
        out_shape=(
            jax.ShapeDtypeStruct((rows, depth), F32),
            jax.ShapeDtypeStruct((rows, depth), BF16),
            jax.ShapeDtypeStruct((8, depth), F32),
            jax.ShapeDtypeStruct((chips, 2, rows, width), BF16),
        ),
        in_specs=[VMEM()] * (5 + len(received)),
        out_specs=(VMEM(),) * 4,
        compiler_params=compiler_params(),
        cost_estimate=cost(
            flops=2 * rows * weights.shape[0] * depth,
            bytes_accessed=2 * weights.shape[0] * depth + 20 * rows * depth,
            transcendentals=0,
        ),
        name="attention_out_back",
    )(kept, *received, middle, gain, weights, grad)


def weights_copies(layer, refs, held, arrived):
    copies = [
        pltpu.make_async_copy(ref.at[layer], held.at[n], arrived.at[n])
        for n, ref in enumerate(refs)
    ]
    for copy in copies:
        copy.start()
    return copies


def feed_kernel(layer, shares, shards, *refs):
    refs = list(refs)
    held, arrived = refs[-2:]
    copies = weights_copies(layer, refs[shares : shares + 3 * shards], held, arrived)
    kept, sent = refs[-4:-2]
    mixed = jnp.concatenate([ref[...] for ref in refs[:shares]], axis=0)
    rows = kept.shape[0]
    total = None
    for at in range(0, 3 * shards, 3):
        copies[at].wait()
        gate = lax.dot_general(mixed, held[at], NT, preferred_element_type=F32)
        copies[at + 1].wait()
        upward = lax.dot_general(mixed, held[at + 1], NT, preferred_element_type=F32)
        hidden = (gate * jax.nn.sigmoid(gate) * upward).astype(BF16)
        copies[at + 2].wait()
        term = jnp.dot(hidden, held[at + 2], preferred_element_type=F32)
        total = term if total is None else total + term
    kept[...] = total[:rows]
    for share in range(1, shares):
        sent[share - 1] = total[share * rows : (share + 1) * rows].astype(BF16)


def held_weights(weights):
    return [
        pltpu.VMEM((len(weights), *weights[0].shape[1:]), BF16),
        pltpu.SemaphoreType.DMA((len(weights),)),
    ]


def feed_forward(layer, blocks, weights):
    shares = len(blocks)
    rows, depth = blocks[0].shape
    units = weights[0].shape[1] * len(weights) // 3
    return pl.pallas_call(
        functools.partial(feed_kernel, layer, shares, len(weights) // 3),
        out_shape=(
            jax.ShapeDtypeStruct((rows, depth), F32),
            jax.ShapeDtypeStruct((shares - 1, rows, depth), BF16),
        ),
        in_specs=[VMEM()] * shares + [pl.BlockSpec(memory_space=pl.ANY)] * len(weights),
        out_specs=(VMEM(),) * 2,
        scratch_shapes=held_weights(weights),
        compiler_params=compiler_params(),
        cost_estimate=cost(
            flops=6 * shares * rows * units * depth,
            bytes_accessed=6 * units * depth,
            transcendentals=shares * rows * units,
        ),
        name="feed_forward",
    )(*blocks, *weights)


def feed_back_kernel(layer, shares, shards, forward, *refs):
    refs = list(refs)
    held, arrived = refs[-2:]
    copies = weights_copies(layer, refs[2 * shares : 2 * shares + 3 * shards], held, arrived)
    mixed = jnp.concatenate([ref[...] for ref in refs[:shares]], axis=0)
    grads = jnp.concatenate([ref[...] for ref in refs[shares : 2 * shares]], axis=0)
    outs = refs[2 * shares + 3 * shards : -2]
    kept, sent = outs[:2]
    rows = kept.shape[0]
    total, forward_total = None, None
    for at in range(0, 3 * shards, 3):
        hidden_out, gate_out, up_out = outs[2 + at : 5 + at]
        copies[at].wait()
        gate = lax.dot_general(mixed, held[at], NT, preferred_element_type=F32)
        copies[at + 1].wait()
        upward = lax.dot_general(mixed, held[at + 1], NT, preferred_element_type=F32)
        sigmoid = jax.nn.sigmoid(gate)
        swish = gate * sigmoid
        hidden = (swish * upward).astype(BF16)
        hidden_out[...] = hidden
        copies[at + 2].wait()
        hidden_grad = lax.dot_general(grads, held[at + 2], NT, preferred_element_type=F32)
        gate_back = (hidden_grad * upward * (sigmoid + swish * (1 - sigmoid))).astype(BF16)
        up_back = (hidden_grad * swish).astype(BF16)
        gate_out[...] = gate_back
        up_out[...] = up_back
        term = jnp.dot(gate_back, held[at], preferred_element_type=F32)
        term = term + jnp.dot(up_back, held[at + 1], preferred_element_type=F32)
        total = term if total is None else total + term
        if forward:
            term = jnp.dot(hidden, held[at + 2], preferred_element_type=F32)
            forward_total = term if forward_total is None else forward_total + term
    kept[...] = total[:rows]
    for share in range(1, shares):
        sent[share - 1] = total[share * rows : (share + 1) * rows].astype(BF16)
    if forward:
        forward_kept, forward_sent = outs[-2:]
        forward_kept[...] = forward_total[:rows]
        for share in range(1, shares):
            forward_sent[share - 1] = forward_total[share * rows : (share + 1) * rows].astype(BF16)


def feed_back(layer, blocks, grads, weights, forward):
    shares = len(blocks)
    rows, depth = blocks[0].shape
    units = weights[0].shape[1]
    wide = jax.ShapeDtypeStruct((shares * rows, units), BF16)
    terms = (
        jax.ShapeDtypeStruct((rows, depth), F32),
        jax.ShapeDtypeStruct((shares - 1, rows, depth), BF16),
    )
    out_shape = terms + (wide,) * len(weights) + (terms if forward else ())
    return pl.pallas_call(
        functools.partial(feed_back_kernel, layer, shares, len(weights) // 3, forward),
        out_shape=out_shape,
        in_specs=[VMEM()] * (2 * shares) + [pl.BlockSpec(memory_space=pl.ANY)] * len(weights),
        out_specs=(VMEM(),) * len(out_shape),
        scratch_shapes=held_weights(weights),
        compiler_params=compiler_params(),
        cost_estimate=cost(
            flops=4 * shares * rows * units * len(weights) * depth,
            bytes_accessed=2 * units * len(weights) * depth,
            transcendentals=shares * rows * units,
        ),
        name="feed_backward",
    )(*blocks, *grads, *weights)


def feed_weights_kernel(shares, added, blocks, *refs):
    refs = list(refs)
    places = refs.pop(0) if blocks else None
    hidden, gate_back, up_back = (refs.pop(0)[...] for _ in range(3))
    mixed = jnp.concatenate([refs.pop(0)[...] for _ in range(shares)], axis=0)
    grads = jnp.concatenate([refs.pop(0)[...] for _ in range(shares)], axis=0)
    received = refs.pop(0) if added else None
    units = hidden.shape[1]
    half = 3 * units // 2
    for index, (left, right) in enumerate(((gate_back, mixed), (up_back, mixed), (hidden, grads))):
        start = index * units
        term = lax.dot_general(left, right, TN, preferred_element_type=F32)
        if added:
            term = term + received[start : start + units, :].astype(F32)
        term = term.astype(BF16)
        if not blocks:
            refs[0][start : start + units, :] = term
            continue
        size = term.shape[1] // blocks
        for part in range(2):
            low, high = max(start, part * half), min(start + units, (part + 1) * half)
            if low >= high:
                continue
            for block in range(blocks):
                piece = term[low - start : high - start, block * size : (block + 1) * size]
                refs[part][block ^ places[part], low - part * half : high - part * half, :] = piece


def feed_weights(activations, mixed, grads, received, places=None, blocks=0):
    shares = len(mixed)
    units = activations[0].shape[1]
    rows, depth = mixed[0].shape
    operands = [*activations, *mixed, *grads] + ([] if received is None else [received])
    specs = [VMEM()] * len(operands)
    if blocks:
        operands = [places] + operands
        specs = [SMEM()] + specs
        out = jax.ShapeDtypeStruct((blocks, 3 * units // 2, depth // blocks), BF16)
        out_shape, out_specs = (out, out), (VMEM(), VMEM())
    else:
        out_shape, out_specs = jax.ShapeDtypeStruct((3 * units, depth), BF16), VMEM()
    return pl.pallas_call(
        functools.partial(feed_weights_kernel, shares, received is not None, blocks),
        out_shape=out_shape,
        in_specs=specs,
        out_specs=out_specs,
        compiler_params=compiler_params(),
        cost_estimate=cost(
            flops=6 * shares * rows * units * depth,
            bytes_accessed=6 * units * depth,
            transcendentals=0,
        ),
        name="feed_weight_grads",
    )(*operands)


def place_kernel(units, places, first, second, summed, *outs):
    layer = pl.program_id(0)

    def write(rows):
        rows = rows.astype(F32)
        for n, out in enumerate(outs):
            out[0] = rows[n * units : (n + 1) * units]

    @pl.when(layer == 0)
    def _():
        write(jnp.concatenate([first[0], second[0]], axis=0))

    @pl.when(layer > 0)
    def _():
        write(summed[0])


def place_feed(places, first, second, summed):
    blocks, half, size = first.shape
    layers = summed.shape[0] + 1
    units = 2 * half // 3
    out = jax.ShapeDtypeStruct((layers, units, blocks * size), F32)

    def part(index):
        return pl.BlockSpec(
            (1, half, size),
            lambda layer, block, places: (
                jnp.where(layer == 0, block ^ places[index], (blocks - 1) ^ places[index]), 0, 0,
            ),
        )

    return pl.pallas_call(
        functools.partial(place_kernel, units),
        out_shape=(out,) * 3,
        grid_spec=pltpu.PrefetchScalarGridSpec(
            num_scalar_prefetch=1,
            grid=(layers, blocks),
            in_specs=[
                part(0),
                part(1),
                pl.BlockSpec(
                    (1, 2 * half, size),
                    lambda layer, block, places: (
                        jnp.maximum(layer - 1, 0), 0, jnp.where(layer == 0, 0, block),
                    ),
                ),
            ],
            out_specs=[
                pl.BlockSpec((1, units, size), lambda layer, block, places: (layer, 0, block))
            ]
            * 3,
        ),
        compiler_params=compiler_params(),
        name="place_feed_grads",
    )(places, first, second, summed)


def head_weights_kernel(raws, *refs):
    out = refs[-1]
    rows = jnp.concatenate([ref[...] for ref in refs[:-1]], axis=0)
    left = raws[...].reshape(rows.shape[0], raws.shape[-1])
    out[...] = lax.dot_general(left, rows, TN, preferred_element_type=F32).astype(BF16)


def head_weights(raws, blocks):
    rows, depth = blocks[0].shape
    wide = raws.shape[-1]
    return pl.pallas_call(
        head_weights_kernel,
        out_shape=jax.ShapeDtypeStruct((wide, depth), BF16),
        in_specs=[VMEM()] * (1 + len(blocks)),
        out_specs=VMEM(),
        compiler_params=compiler_params(),
        cost_estimate=cost(
            flops=2 * len(blocks) * rows * wide * depth,
            bytes_accessed=2 * len(blocks) * rows * (wide + depth),
            transcendentals=0,
        ),
        name="head_weight_grads",
    )(raws, *blocks)


def attend_kernel(chips, rows, width, *refs):
    ids, queries, keys, values, attended, log_totals = refs
    heads = width // HEAD_DIM
    count = 2 * chips * rows
    units = max(count // SEQ_UNIT, 1)
    unit_rows = count // units
    for block in range(2 * chips):
        first = block * rows
        own_unit = first // unit_rows
        segments = [(unit * unit_rows, unit_rows, unit, False) for unit in range(own_unit)]
        if first > own_unit * unit_rows:
            segments.append((own_unit * unit_rows, first - own_unit * unit_rows, None, False))
        segments.append((first, rows, None, True))
        query_all = queries[first : first + rows, :]
        outs = None
        lane = lax.broadcasted_iota(jnp.int32, (rows, 128), 1)
        totals_wide = jnp.zeros((rows, 128), F32)
        for head in range(heads):
            query = head_masked(query_all, head)
            scores, biases, tops = [], [], []
            for start, length, unit, diagonal in segments:
                score = lax.dot_general(
                    query, keys[start : start + length, :], NT, preferred_element_type=F32
                )
                if diagonal:
                    row = lax.broadcasted_iota(jnp.int32, score.shape, 0)
                    column = lax.broadcasted_iota(jnp.int32, score.shape, 1)
                    score = jnp.where(column <= row, score, NEG_LARGE)
                bias = 0.0
                if unit is not None:
                    bias = jnp.where(ids[2 + own_unit * units + unit] > 0, 0.0, NEG_LARGE)
                scores.append(score)
                biases.append(bias)
                tops.append(jnp.max(score, axis=1, keepdims=True) + bias)
            highest = functools.reduce(jnp.maximum, tops)
            summed, total = None, None
            for (start, length, unit, diagonal), score, bias in zip(segments, scores, biases):
                weight = jnp.exp(score - (highest - bias))
                narrow = weight.astype(BF16)
                value = values[start : start + length, :]
                if heads > 1:
                    value_lane = lax.broadcasted_iota(jnp.int32, value.shape, 1)
                    value = jnp.where(value_lane // HEAD_DIM == head, value, jnp.ones_like(value))
                else:
                    part_total = jnp.sum(weight, axis=1, keepdims=True)
                    total = part_total if total is None else total + part_total
                product = jnp.dot(narrow, value, preferred_element_type=F32)
                summed = product if summed is None else summed + product
            if heads > 1:
                spread = pltpu.roll(summed, HEAD_DIM, 1)
                divided = head_masked(summed / spread, head)
                total = jnp.where(lane // HEAD_DIM == head, spread, summed)
                logs = highest + jnp.log(total)
            else:
                divided = summed / total
                logs = jnp.broadcast_to(highest + jnp.log(total), (rows, 128))
            outs = divided if outs is None else outs + divided
            totals_wide = jnp.where(lane == head, logs, totals_wide)
        attended[(block % chips) ^ ids[0], (block // chips) ^ ids[1]] = outs.astype(BF16)
        log_totals[:, first : first + rows] = totals_wide.T[:8]


def attend(ids, queries, keys, values, chips, rows):
    count, width = queries.shape
    heads = width // HEAD_DIM
    pairs = count * count // 2
    return pl.pallas_call(
        functools.partial(attend_kernel, chips, rows, width),
        out_shape=(
            jax.ShapeDtypeStruct((chips, 2, rows, width), BF16),
            jax.ShapeDtypeStruct((8, count), F32),
        ),
        in_specs=[SMEM()] + [VMEM()] * 3,
        out_specs=(VMEM(),) * 2,
        compiler_params=compiler_params(),
        cost_estimate=cost(
            flops=heads * pairs * 256 * 8,
            bytes_accessed=2 * count * width * 4,
            transcendentals=heads * pairs,
        ),
        name="attend_forward",
    )(ids, queries, keys, values)


def attend_back_kernel(chips, rows, width, layer_first, *refs):
    refs = list(refs)
    ids, queries, keys, values, attended = (refs.pop(0) for _ in range(5))
    near = [refs.pop(0) for _ in range(chips)]
    far, log_totals, cosine, sine = (refs.pop(0) for _ in range(4))
    later_layer = refs.pop(0) if layer_first else None
    outs, grad_rows, inner, query_total, key_total, value_total = refs
    heads = width // HEAD_DIM
    count = 2 * chips * rows
    units = max(count // SEQ_UNIT, 1)
    unit_rows = count // units

    for core in range(2):
        for chip in range(chips):
            at = place_of(ids, core, chip, chips, rows)
            grad = near[chip][0] if core == 0 else far[chip]
            grad_rows[at, :] = grad
            query_total[at, :] = grad.astype(F32) * attended[chip, core].astype(F32)
    turned = query_total[...].T
    for head in range(heads):
        inner[head : head + 1, :] = jnp.sum(
            turned[head * HEAD_DIM : (head + 1) * HEAD_DIM], axis=0, keepdims=True
        )
    query_total[...] = jnp.zeros_like(query_total)
    key_total[...] = jnp.zeros_like(key_total)
    value_total[...] = jnp.zeros_like(value_total)

    def work(key_start, key_count, query_start, diagonal):
        at = pl.ds(key_start, key_count)
        query_at = pl.ds(query_start, rows)
        key, value = keys[at, :], values[at, :]
        key_part, value_part, query_part = None, None, None
        for head in range(heads):
            query = head_masked(queries[query_at, :], head)
            grad = head_masked(grad_rows[query_at, :], head)
            score = lax.dot_general(key, query, NT, preferred_element_type=F32)
            weight = jnp.exp(score - log_totals[head : head + 1, query_at])
            if diagonal:
                row = lax.broadcasted_iota(jnp.int32, score.shape, 0)
                column = lax.broadcasted_iota(jnp.int32, score.shape, 1)
                weight = jnp.where(row <= column, weight, 0.0)
            back = lax.dot_general(value, grad, NT, preferred_element_type=F32)
            score_back = (weight * (back - inner[head : head + 1, query_at])).astype(BF16)
            narrow = weight.astype(BF16)
            value_term = jnp.dot(narrow, grad, preferred_element_type=F32)
            key_term = jnp.dot(score_back, query, preferred_element_type=F32)
            query_term = lax.dot_general(
                score_back, head_masked(key, head), TN, preferred_element_type=F32
            )
            if head == 0:
                key_part, value_part, query_part = key_term, value_term, query_term
            else:
                key_part, value_part, query_part = (
                    key_part + key_term, value_part + value_term, query_part + query_term,
                )
        key_total[at, :] += key_part
        value_total[at, :] += value_part
        query_total[query_at, :] += query_part

    for unit in range(units):
        start = unit * unit_rows
        blocks = unit_rows // rows
        for other in range(unit):
            @pl.when(ids[2 + unit * units + other] > 0)
            def _():
                @pl.loop(0, blocks)
                def _(index):
                    at = pl.multiple_of(start + index * rows, rows)
                    work(other * unit_rows, unit_rows, at, False)
        for index in range(blocks):
            if index:
                work(start, index * rows, start + index * rows, False)
            work(start + index * rows, rows, start + index * rows, True)

    for core in range(2):
        for chip in range(chips):
            at = place_of(ids, core, chip, chips, rows)
            turn_at = table_rows(ids, core, chip, chips, rows)
            cos, sin = cosine[turn_at, :], sine[turn_at, :]
            query = query_total[at, :] * HEAD_DIM**-0.5
            key = key_total[at, :]
            value = value_total[at, :]
            query = query * cos - half_turn(query) * sin
            key = key * cos - half_turn(key) * sin
            if layer_first:
                value = value + later_layer[core, chip, :, 2 * width :].astype(F32)
            else:
                value = value.astype(BF16).astype(F32) * 0.5
            outs[core, chip] = jnp.concatenate([query, key, value], axis=1).astype(BF16)


def attend_back(
    ids, queries, keys, values, attended, near, far, log_totals, cosine, sine, later_layer
):
    chips, _, rows, width = attended.shape
    count = queries.shape[0]
    heads = width // HEAD_DIM
    pairs = count * count // 2
    operands = [ids, queries, keys, values, attended, *near, far, log_totals, cosine, sine]
    if later_layer is not None:
        operands.append(later_layer)
    return pl.pallas_call(
        functools.partial(attend_back_kernel, chips, rows, width, later_layer is not None),
        out_shape=jax.ShapeDtypeStruct((2, chips, rows, 3 * width), BF16),
        in_specs=[SMEM()] + [VMEM()] * (len(operands) - 1),
        out_specs=VMEM(),
        scratch_shapes=[
            pltpu.VMEM((count, width), BF16),
            pltpu.VMEM((8, count), F32),
            pltpu.VMEM((count, width), F32),
            pltpu.VMEM((count, width), F32),
            pltpu.VMEM((count, width), F32),
        ],
        compiler_params=compiler_params(),
        cost_estimate=cost(
            flops=heads * pairs * 256 * 20,
            bytes_accessed=2 * count * width * 20,
            transcendentals=heads * pairs,
        ),
        name="attend_backward",
    )(*operands)


def rms_factor(values):
    return lax.rsqrt(jnp.mean(values * values, axis=-1, keepdims=True) + EPSILON)


def normed_rows(values, gain):
    return (values * rms_factor(values) * gain).astype(BF16)


def norm_back(values, gain, back):
    factor = rms_factor(values)
    scaled = back * gain
    mean = jnp.mean(scaled * values, axis=-1, keepdims=True)
    gain_grad = jnp.sum(back * values * factor, axis=0)
    return factor * scaled - values * (factor * factor * factor * mean), gain_grad


def matmul(left, right):
    return jnp.dot(left, right, preferred_element_type=F32)


def matmul_nt(left, right):
    return lax.dot_general(left, right, NT, preferred_element_type=F32)


def matmul_tn(left, right):
    return lax.dot_general(left, right, TN, preferred_element_type=F32)


def flat(blocks):
    return blocks.reshape(-1, blocks.shape[-1])


def per_device(
    head_axes, hid_axes, inputs, cotangent, segments, attn_gain, w_query, w_key, w_value, w_out,
    mlp_gain, w_gate, w_up, w_down,
):
    layers = w_query.shape[0]
    core = hid_axes[-1]
    group_axes = head_axes[1:]
    share_axes = hid_axes[:-1]
    chips = 2 ** len(group_axes)
    rows = inputs.shape[0]
    count = 2 * chips * rows
    width = w_query.shape[2]
    units = max(count // SEQ_UNIT, 1)
    share_at = lax.axis_index(share_axes[0])

    def index_of(axes):
        at = jnp.int32(0)
        for axis in axes:
            at = at * 2 + lax.axis_index(axis)
        return at

    def turn(value):
        return lax.ppermute(value, (head_axes[0], core), TURN)

    unit_axes = ((core,) + group_axes)[: (units - 1).bit_length()]
    number = turn(jnp.broadcast_to(segments[:1], (8, 128)))
    unit_at = index_of(unit_axes)
    def group_ids(number):
        numbers = jnp.stack(
            [number] + [swap(number, axes_of(i, unit_axes)) for i in range(1, units)]
        )[:, 0, 0]
        numbers = jnp.stack(
            [lax.dynamic_index_in_dim(numbers, unit ^ unit_at, 0, False) for unit in range(units)]
        )
        same = (numbers[:, None] == numbers[None, :]).astype(jnp.int32)
        places = jnp.stack([index_of(group_axes), lax.axis_index(core)]).astype(jnp.int32)
        earlier_units = np.tril(np.ones((units, units), np.int32), -1)
        starts = jnp.sum(same * earlier_units, axis=1) * SEQ_UNIT
        return jnp.concatenate([places, same.reshape(-1), starts])

    feed_orders = (head_axes[::-1], (head_axes[1], *head_axes[:1:-1], head_axes[0]))
    feed_places = jnp.stack([index_of(order) for order in feed_orders]).astype(jnp.int32)
    frequency = np.float32(THETA) ** (-np.arange(HEAD_DIM // 2, dtype=np.float32) * 2 / HEAD_DIM)
    frequency = np.tile(frequency.astype(np.float32), 2 * width // HEAD_DIM)[None]
    signs = np.where(np.arange(width) % HEAD_DIM < HEAD_DIM // 2, -1.0, 1.0).astype(np.float32)
    angles = jnp.arange(count, dtype=jnp.int32).astype(F32)[:, None] * frequency
    cosine, sine = jnp.cos(angles), jnp.sin(angles) * signs

    feed_all = (w_gate.transpose(0, 2, 1), w_up.transpose(0, 2, 1), w_down)

    def joined_shares(piece):
        other = swap(piece, share_axes[:1])
        return jnp.where(
            share_at == 0,
            jnp.concatenate([piece, other], axis=0),
            jnp.concatenate([other, piece], axis=0),
        )

    packed = pack_heads(share_at[None].astype(jnp.int32), (w_query, w_key, w_value, w_out))

    def add_received(total, sent):
        for i in range(1, 1 + sent.shape[0]):
            total = total + swap(sent[i - 1], axes_of(i, share_axes)).astype(F32)
        return total

    attn_gains = [attn_gain[n][None] for n in range(layers)]
    mlp_gains = [mlp_gain[n][None] for n in range(layers)]
    residual = turn(inputs)
    w_heads = [turn(packed[0])] + [None] * (layers - 1)
    residual, cosine, sine, w_heads[0] = lax.optimization_barrier(
        (residual, cosine, sine, w_heads[0])
    )
    residual = residual.astype(F32)
    w_outs = [None] * layers

    stored = []
    first_values = None
    for layer in range(layers):
        final = layer == layers - 1
        before = residual
        w_heads[layer] = joined_shares(after(w_heads[layer], before))
        near, far = gather(
            normed_rows(before, attn_gains[layer]), group_axes, core, w_heads[layer]
        )
        blocks = near + far
        if layer == 0:
            ids = group_ids(after(number, near[1]))
        queries, keys, values = project(ids, blocks, w_heads[layer], cosine, sine, first_values)
        if layer == 0:
            first_values = values
            feeds = [swap(after(w, queries), (core,)) for w in feed_all[:2]]
        out_chips = gather_chips(after(w_heads[layer][3 * width :], queries), group_axes)
        attended, log_totals = attend(ids, queries, keys, values, chips, rows)
        attended = after(attended, *out_chips[1:], *(feeds if layer == 0 else ()))
        if layer == 1:
            down_in = gather_chips(after(grad, queries), share_axes)
        near, far = exchange(attended, group_axes, core)
        out_chips = after(jnp.concatenate(out_chips, axis=0), near[-1])
        w_outs[layer] = jnp.concatenate([out_chips, swap(out_chips, (core,))], axis=0)
        if layer == 0:
            feeds.append(swap(after(feed_all[2], far), (core,)))
            feed_all = feed_all + tuple(feeds)
            grad = turn(after(cotangent, far))
        if layer == 1:
            far = after(far, down_in[-1])
        attended_rows, middle, normed = middle_step(
            near, far, w_outs[layer], before, mlp_gains[layer]
        )
        mixed = gather_chips(normed, share_axes)
        stored.append(
            dict(
                before=before, blocks=blocks, queries=queries, keys=keys, values=values,
                attended=attended, log_totals=log_totals, attended_rows=attended_rows,
                middle=middle, mixed=mixed,
            )
        )
        if not final:
            w_heads[layer + 1] = turn(after(packed[layer + 1], far))
            first_mixed = after(mixed[0], w_heads[layer + 1])
            own_term, sent = feed_forward(layer, [first_mixed] + mixed[1:], feed_all)
            residual = add_received(middle + own_term, sent)
            if layer == 0:
                residual = after(residual, grad)

    grad = grad.astype(F32)
    attn_grads, mlp_grads = [], []
    attn_gain_grads, mlp_gain_grads = [], []
    later_layer = None
    by_blocks = inputs.shape[1] % (128 * 2 ** len(head_axes)) == 0
    for layer in reversed(range(layers)):
        final = layer == layers - 1
        k = stored[layer]
        mixed = k["mixed"]
        if not final:
            down_in = gather_chips(grad.astype(BF16), share_axes)
        own_term, sent, *rest = feed_back(layer, mixed, down_in, feed_all, final)
        received = [swap(sent[i - 1], axes_of(i, share_axes)) for i in range(1, len(mixed))]
        other = swap(feed_weights(rest[3:6], mixed, down_in, None), (core,))
        ties = ()
        if layer:
            mlp_part = feed_weights(rest[:3], mixed, down_in, other)
            block = lax.psum_scatter(mlp_part, head_axes, scatter_dimension=0, tiled=True)
            mlp_grads.append(block)
            mlp_part = (mlp_part,)
        elif by_blocks:
            mlp_part = feed_weights(
                rest[:3], mixed, down_in, other, feed_places, 2 ** len(head_axes)
            )
            half = mlp_part[0].shape[0] // 2
            ties = [swap(p[half:], order[:1]) for p, order in zip(mlp_part, feed_orders)]
        else:
            mlp_part = (feed_weights(rest[:3], mixed, down_in, other),)
            mlp_grads.append(lax.psum(mlp_part[0], head_axes[::-1]))
        if not final:
            own_term = after(own_term, mlp_grads[0])
            mlp_grads[0] = lax.all_gather(mlp_grads[0], head_axes, axis=0, tiled=True)
        middle_back, attn_in, gain_part, heads_back = middle_back_step(
            own_term, received, k["middle"], mlp_gains[layer], w_outs[layer], grad, chips
        )
        mlp_gain_grads.append(gain_part[0])
        near, far = exchange(heads_back, group_axes, core)
        if final:
            block_out = add_received(k["middle"] + rest[6], after(rest[7], far)).astype(BF16)
        raws = attend_back(
            ids, after(k["queries"], *mlp_part), k["keys"], k["values"], k["attended"], near, far,
            k["log_totals"], cosine, sine, later_layer,
        )
        later_layer = raws
        into = w_heads[layer][: 3 * width]
        others = matmul(flat(raws[1]), into).astype(BF16).reshape(chips, rows, -1)
        mine = matmul(flat(raws[0]), into).reshape(chips, rows, -1)
        normed_in = scatter_sum(mine, others, group_axes, core, *ties)
        part, gain_part = norm_back(k["before"], attn_gains[layer], normed_in)
        attn_gain_grads.append(gain_part)
        grad = middle_back + part
        if not final:
            grad = after(grad, mlp_grads[0])
        attn_in = after(attn_in, grad)
        out_terms = matmul_tn(k["attended_rows"], attn_in).reshape(2, chips, width, -1)
        out_grad = scatter_sum(out_terms[0], out_terms[1].astype(BF16), group_axes, core)
        heads_grad = head_weights(after(raws, grad), k["blocks"])
        attn_grads.append(jnp.concatenate([heads_grad, out_grad.astype(BF16)], axis=0))

    joined = jnp.stack(attn_grads[::-1], axis=1)
    kept_part = lax.dynamic_slice_in_dim(joined, share_at * 2 * width, 2 * width, 0)
    sent_part = lax.dynamic_slice_in_dim(joined, (1 - share_at) * 2 * width, 2 * width, 0)
    summed = kept_part.astype(F32) + swap(sent_part, share_axes[:1]).astype(F32)
    summed = exchange_sum(turn(summed.astype(BF16)), (core,) + share_axes[1:])
    attn_all = joined_shares(summed).astype(F32).transpose(1, 0, 2)

    given = turn(jnp.stack([block_out, grad.astype(BF16)]))
    gains = exchange_sum(
        jnp.stack(attn_gain_grads[::-1] + mlp_gain_grads[::-1]), hid_axes[::-1] + head_axes, F32
    )
    if by_blocks:
        spread = [
            spread_blocks(reduce_blocks(part[:half], received, order), order)
            for part, received, order in zip(mlp_part, ties, feed_orders)
        ]
        feed_grads = place_feed(feed_places, *spread, jnp.stack(mlp_grads[::-1]))
    else:
        mlp_all = jnp.stack(mlp_grads[::-1]).astype(F32)
        size = w_gate.shape[2]
        feed_grads = [mlp_all[:, n * size : (n + 1) * size] for n in range(3)]
    return (
        given[0],
        given[1].astype(F32),
        gains[:layers],
        attn_all[:, :width].transpose(0, 2, 1),
        attn_all[:, width : 2 * width].transpose(0, 2, 1),
        attn_all[:, 2 * width : 3 * width].transpose(0, 2, 1),
        attn_all[:, 3 * width :],
        gains[layers:],
        feed_grads[0].transpose(0, 2, 1),
        feed_grads[1].transpose(0, 2, 1),
        feed_grads[2],
    )


def solution(mesh):
    head_bits = (mesh.shape["heads"] - 1).bit_length()
    hid_bits = (mesh.shape["hid"] - 1).bit_length()
    head_axes = tuple(f"heads{n}" for n in range(head_bits))
    hid_axes = tuple(f"hid{n}" for n in range(hid_bits))
    binary = Mesh(mesh.devices.reshape((2,) * (head_bits + hid_bits)), head_axes + hid_axes)
    tokens = hid_axes + head_axes
    in_specs = (
        P(tokens, None),
        P(tokens, None),
        P(tokens),
        P(),
        P(None, None, head_axes),
        P(None, None, head_axes),
        P(None, None, head_axes),
        P(None, head_axes, None),
        P(),
        P(None, None, hid_axes),
        P(None, None, hid_axes),
        P(None, hid_axes, None),
    )
    out_specs = (
        P(tokens, None),
        P(tokens, None),
        P(),
        P(None, None, head_axes),
        P(None, None, head_axes),
        P(None, None, head_axes),
        P(None, head_axes, None),
        P(),
        P(None, None, hid_axes),
        P(None, None, hid_axes),
        P(None, hid_axes, None),
    )
    return jax.shard_map(
        functools.partial(per_device, head_axes, hid_axes),
        mesh=binary,
        in_specs=in_specs,
        out_specs=out_specs,
        check_vma=False,
    )
```

```python
import functools

import jax
import jax.numpy as jnp
import numpy as np
from jax import lax
from jax.experimental import pallas as pl
from jax.experimental.pallas import tpu as pltpu
from jax.sharding import Mesh
from jax.sharding import PartitionSpec as P

HEAD_DIM = 64
SEQ_UNIT = 1024
EPSILON = 1e-06
THETA = 10000.0
NEG_LARGE = -1e30
BF16 = jnp.bfloat16
F32 = jnp.float32
VMEM_BYTES = 36 * 1024 * 1024
SCALE = 0.2
WIDE = 2.0

NT = (((1,), (1,)), ((), ()))
TN = (((0,), (0,)), ((), ()))


def swap(value, axes):
    axes = tuple(sorted(axes))
    size = 2 ** len(axes)
    return lax.ppermute(
        value, axes if len(axes) > 1 else axes[0], [(i, size - 1 - i) for i in range(size)]
    )


def axes_of(bits, axes):
    count = len(axes)
    return tuple(a for n, a in enumerate(axes) if bits >> (count - 1 - n) & 1)


def gather_chips(value, axes):
    return [value] + [swap(value, axes_of(i, axes)) for i in range(1, 2 ** len(axes))]


def after(value, *others):
    return lax.optimization_barrier((value, *others))[0]


def gather(value, axes, core, *ties):
    if len(axes) == 2:
        half = value.shape[-1] // 2
        own = swap(value, (core,))
        low = swap(value, axes[1:])
        high = swap(value, axes[:1])
        low, high, own, *_ = lax.optimization_barrier((low, high, own, *ties))
        both = jnp.concatenate(
            [swap(low[..., :half], axes[:1]), swap(high[..., half:], axes[1:])], axis=-1
        )
        chips = [value, low, high, both]
        return chips, [own] + [swap(c, (core,)) for c in chips[1:]]
    chips = gather_chips(value, axes)
    return chips, [swap(c, (core,)) for c in chips]


class BlockSum:
    def __init__(self, parts, axes):
        self.axes, self.done = axes, 0
        half = parts.shape[0] // 2
        self.kept, self.sent = parts[:half], parts[half:]

    def step(self, *ties):
        count = len(self.axes)
        if self.done < count:
            received = swap(after(self.sent, *ties), (self.axes[self.done],))
            total = (self.kept.astype(F32) + received.astype(F32)).astype(BF16)
            half = total.shape[0] // 2
            self.kept, self.sent = (total[:half], total[half:]) if half else (total, None)
        else:
            block = after(self.kept, *ties)
            received = swap(block, (self.axes[2 * count - 1 - self.done],))
            self.kept = jnp.concatenate([block, received], axis=0)
        self.done += 1
        return received


def steps(sums, *ties):
    return [part.step(*ties) for part in sums]


def scatter_sum(mine, others, axes, core, *ties):
    mine = mine + swap(others, (core,)).astype(F32)
    sent = after(mine.astype(BF16), *ties)
    total = mine[0]
    for i in range(1, 2 ** len(axes)):
        total = total + swap(sent[i], axes_of(i, axes)).astype(F32)
    return total


def exchange(blocks, axes, core):
    got = [blocks[0]] + [swap(blocks[i], axes_of(i, axes)) for i in range(1, 2 ** len(axes))]
    return got, swap(jnp.stack([g[1] for g in got]), (core,))


def exchange_sum(value, axes, kind=BF16):
    for axis in axes:
        value = (value.astype(F32) + swap(value, (axis,)).astype(F32)).astype(kind)
    return value


TURN = [(0, 0), (1, 2), (2, 1), (3, 3)]


def compiler_params():
    return pltpu.CompilerParams(vmem_limit_bytes=VMEM_BYTES)


def cost(flops, bytes_accessed, transcendentals, scale=SCALE):
    return pl.CostEstimate(
        flops=int(flops * scale),
        bytes_accessed=int(bytes_accessed * scale),
        transcendentals=int(transcendentals * scale),
    )


VMEM = functools.partial(pl.BlockSpec, memory_space=pltpu.VMEM)
SMEM = functools.partial(pl.BlockSpec, memory_space=pltpu.SMEM)


def half_turn(value):
    width = value.shape[-1]
    halfway = HEAD_DIM // 2
    if width == HEAD_DIM:
        return jnp.concatenate([value[:, halfway:], value[:, :halfway]], axis=-1)
    lane = lax.broadcasted_iota(jnp.int32, value.shape, 1)
    return jnp.where(
        lane % HEAD_DIM < halfway,
        pltpu.roll(value, width - halfway, 1),
        pltpu.roll(value, halfway, 1),
    )


def head_masked(value, head):
    if value.shape[-1] == HEAD_DIM:
        return value
    lane = lax.broadcasted_iota(jnp.int32, value.shape, 1)
    return jnp.where(lane // HEAD_DIM == head, value, jnp.zeros_like(value))


def place_of(ids, core, chip, chips, rows):
    place = (core ^ ids[1]) * chips + (chip ^ ids[0])
    return pl.ds(pl.multiple_of(place * rows, rows), rows)


def pack_kernel(width, places, *refs):
    out = refs[-1]
    layers = out.shape[0]
    for layer in range(layers):
        for half in range(2):
            @pl.when(places[0] == half)
            def _():
                for n in range(2):
                    part = refs[2 * half + n][layer]
                    out[layer, n * width : (n + 1) * width] = part if half and n else part.T


def pack_heads(places, weights):
    layers, depth, width = weights[0].shape
    return pl.pallas_call(
        functools.partial(pack_kernel, width),
        out_shape=jax.ShapeDtypeStruct((layers, 2 * width, depth), BF16),
        in_specs=[SMEM()] + [VMEM()] * 4,
        out_specs=VMEM(),
        compiler_params=compiler_params(),
        cost_estimate=cost(
            flops=0, bytes_accessed=12 * layers * width * depth, transcendentals=0
        ),
        name="pack_head_weights",
    )(places, *weights)


def table_rows(ids, core, chip, chips, rows):
    count = 2 * chips * rows
    units = max(count // SEQ_UNIT, 1)
    first = ((core ^ ids[1]) * chips + (chip ^ ids[0])) * rows
    unit = first // (count // units)
    start = ids[2 + units * units + unit]
    return pl.ds(pl.multiple_of(start + first % (count // units), rows), rows)


def project_kernel(mixed, chips, rows, width, *refs):
    refs = list(refs)
    ids = refs.pop(0)
    blocks = [refs.pop(0) for _ in range(2 * chips)]
    weights, cosine, sine = (refs.pop(0) for _ in range(3))
    first = refs.pop(0) if mixed else None
    queries, keys, values = refs
    for number, block in enumerate(blocks):
        raw = lax.dot_general(block[...], weights[: 3 * width, :], NT, preferred_element_type=F32)
        at = place_of(ids, number // chips, number % chips, chips, rows)
        query, key, value = (raw[:, n * width : (n + 1) * width] for n in range(3))
        turn_at = table_rows(ids, number // chips, number % chips, chips, rows)
        cos, sin = cosine[turn_at, :], sine[turn_at, :]
        queries[at, :] = ((query * cos + half_turn(query) * sin) * HEAD_DIM**-0.5).astype(BF16)
        keys[at, :] = (key * cos + half_turn(key) * sin).astype(BF16)
        if mixed:
            value = 0.5 * value + 0.5 * first[at, :].astype(F32)
        values[at, :] = value.astype(BF16)


def project(ids, blocks, weights, cosine, sine, first):
    chips = len(blocks) // 2
    rows, depth = blocks[0].shape
    width = weights.shape[0] // 4
    count = 2 * chips * rows
    out = jax.ShapeDtypeStruct((count, width), BF16)
    operands = (ids, *blocks, weights, cosine, sine) + (() if first is None else (first,))
    return pl.pallas_call(
        functools.partial(project_kernel, first is not None, chips, rows, width),
        out_shape=(out, out, out),
        in_specs=[SMEM()] + [VMEM()] * (len(operands) - 1),
        out_specs=(VMEM(),) * 3,
        compiler_params=compiler_params(),
        cost_estimate=cost(
            flops=2 * count * depth * 3 * width,
            bytes_accessed=2 * count * depth + 6 * depth * width + 14 * count * width,
            transcendentals=0,
        ),
        name="project_heads",
    )(*operands)


def lanes_joined(pieces):
    return jnp.concatenate(pieces, axis=1)


def middle_kernel(chips, *refs):
    refs = list(refs)
    near = [refs.pop(0) for _ in range(chips)]
    far, weights, before, gain, attended_rows, middle, normed = refs
    rows = lanes_joined([n[0] for n in near] + [far[i] for i in range(chips)])
    attended_rows[...] = rows
    value = before[...] + jnp.dot(rows, weights[...], preferred_element_type=F32)
    middle[...] = value
    normed[...] = normed_rows(value, gain[...])


def middle_step(near, far, weights, before, gain):
    chips = len(near)
    rows, depth = before.shape
    features = weights.shape[0]
    return pl.pallas_call(
        functools.partial(middle_kernel, chips),
        out_shape=(
            jax.ShapeDtypeStruct((rows, features), BF16),
            jax.ShapeDtypeStruct((rows, depth), F32),
            jax.ShapeDtypeStruct((rows, depth), BF16),
        ),
        in_specs=[VMEM()] * (chips + 4),
        out_specs=(VMEM(),) * 3,
        compiler_params=compiler_params(),
        cost_estimate=cost(
            flops=2 * rows * features * depth,
            bytes_accessed=2 * features * depth + 14 * rows * depth,
            transcendentals=0,
        ),
        name="attention_out",
    )(*near, far, weights, before, gain)


def middle_back_kernel(chips, width, *refs):
    refs = list(refs)
    kept = refs.pop(0)
    middle, gain, weights, grad = refs[-8:-4]
    received = refs[:-8]
    total, rounded, gain_part, blocks = refs[-4:]
    back = kept[...]
    for term in received:
        back = back + term[...].astype(F32)
    part, gains = norm_back(middle[...], gain[...], back)
    value = grad[...] + part
    total[...] = value
    narrow = value.astype(BF16)
    rounded[...] = narrow
    gain_part[...] = jnp.broadcast_to(gains, gain_part.shape)
    heads = lax.dot_general(narrow, weights[...], NT, preferred_element_type=F32).astype(BF16)
    for core in range(2):
        for chip in range(chips):
            at = (core * chips + chip) * width
            blocks[chip, core] = heads[:, at : at + width]


def middle_back_step(kept, received, middle, gain, weights, grad, chips):
    rows, depth = middle.shape
    width = weights.shape[0] // (2 * chips)
    return pl.pallas_call(
        functools.partial(middle_back_kernel, chips, width),
        out_shape=(
            jax.ShapeDtypeStruct((rows, depth), F32),
            jax.ShapeDtypeStruct((rows, depth), BF16),
            jax.ShapeDtypeStruct((8, depth), F32),
            jax.ShapeDtypeStruct((chips, 2, rows, width), BF16),
        ),
        in_specs=[VMEM()] * (5 + len(received)),
        out_specs=(VMEM(),) * 4,
        compiler_params=compiler_params(),
        cost_estimate=cost(
            flops=2 * rows * weights.shape[0] * depth,
            bytes_accessed=2 * weights.shape[0] * depth + 20 * rows * depth,
            transcendentals=0,
        ),
        name="attention_out_back",
    )(kept, *received, middle, gain, weights, grad)


def weights_copies(layer, refs, held, arrived):
    copies = [
        pltpu.make_async_copy(ref.at[layer], held.at[n], arrived.at[n])
        for n, ref in enumerate(refs)
    ]
    for copy in copies:
        copy.start()
    return copies


def feed_kernel(layer, shares, shards, *refs):
    refs = list(refs)
    held, arrived = refs[-2:]
    copies = weights_copies(layer, refs[shares : shares + 3 * shards], held, arrived)
    kept, sent = refs[-4:-2]
    mixed = jnp.concatenate([ref[...] for ref in refs[:shares]], axis=0)
    rows = kept.shape[0]
    total = None
    for at in range(0, 3 * shards, 3):
        copies[at].wait()
        gate = lax.dot_general(mixed, held[at], NT, preferred_element_type=F32)
        copies[at + 1].wait()
        upward = lax.dot_general(mixed, held[at + 1], NT, preferred_element_type=F32)
        hidden = (gate * jax.nn.sigmoid(gate) * upward).astype(BF16)
        copies[at + 2].wait()
        term = jnp.dot(hidden, held[at + 2], preferred_element_type=F32)
        total = term if total is None else total + term
    kept[...] = total[:rows]
    for share in range(1, shares):
        sent[share - 1] = total[share * rows : (share + 1) * rows].astype(BF16)


def held_weights(weights):
    return [
        pltpu.VMEM((len(weights), *weights[0].shape[1:]), BF16),
        pltpu.SemaphoreType.DMA((len(weights),)),
    ]


def feed_forward(layer, blocks, weights):
    shares = len(blocks)
    rows, depth = blocks[0].shape
    units = weights[0].shape[1] * len(weights) // 3
    return pl.pallas_call(
        functools.partial(feed_kernel, layer, shares, len(weights) // 3),
        out_shape=(
            jax.ShapeDtypeStruct((rows, depth), F32),
            jax.ShapeDtypeStruct((shares - 1, rows, depth), BF16),
        ),
        in_specs=[VMEM()] * shares + [pl.BlockSpec(memory_space=pl.ANY)] * len(weights),
        out_specs=(VMEM(),) * 2,
        scratch_shapes=held_weights(weights),
        compiler_params=compiler_params(),
        cost_estimate=cost(
            flops=6 * shares * rows * units * depth,
            bytes_accessed=6 * units * depth,
            transcendentals=shares * rows * units,
        ),
        name="feed_forward",
    )(*blocks, *weights)


def feed_back_kernel(layer, shares, shards, forward, *refs):
    refs = list(refs)
    held, arrived = refs[-2:]
    copies = weights_copies(layer, refs[2 * shares : 2 * shares + 3 * shards], held, arrived)
    mixed = jnp.concatenate([ref[...] for ref in refs[:shares]], axis=0)
    grads = jnp.concatenate([ref[...] for ref in refs[shares : 2 * shares]], axis=0)
    outs = refs[2 * shares + 3 * shards : -2]
    kept, sent = outs[:2]
    rows = kept.shape[0]
    total, forward_total = None, None
    for at in range(0, 3 * shards, 3):
        hidden_out, gate_out, up_out = outs[2 + at : 5 + at]
        copies[at].wait()
        gate = lax.dot_general(mixed, held[at], NT, preferred_element_type=F32)
        copies[at + 1].wait()
        upward = lax.dot_general(mixed, held[at + 1], NT, preferred_element_type=F32)
        sigmoid = jax.nn.sigmoid(gate)
        swish = gate * sigmoid
        hidden = (swish * upward).astype(BF16)
        hidden_out[...] = hidden
        copies[at + 2].wait()
        hidden_grad = lax.dot_general(grads, held[at + 2], NT, preferred_element_type=F32)
        gate_back = (hidden_grad * upward * (sigmoid + swish * (1 - sigmoid))).astype(BF16)
        up_back = (hidden_grad * swish).astype(BF16)
        gate_out[...] = gate_back
        up_out[...] = up_back
        term = jnp.dot(gate_back, held[at], preferred_element_type=F32)
        term = term + jnp.dot(up_back, held[at + 1], preferred_element_type=F32)
        total = term if total is None else total + term
        if forward:
            term = jnp.dot(hidden, held[at + 2], preferred_element_type=F32)
            forward_total = term if forward_total is None else forward_total + term
    kept[...] = total[:rows]
    for share in range(1, shares):
        sent[share - 1] = total[share * rows : (share + 1) * rows].astype(BF16)
    if forward:
        forward_kept, forward_sent = outs[-2:]
        forward_kept[...] = forward_total[:rows]
        for share in range(1, shares):
            forward_sent[share - 1] = forward_total[share * rows : (share + 1) * rows].astype(BF16)


def feed_back(layer, blocks, grads, weights, forward):
    shares = len(blocks)
    rows, depth = blocks[0].shape
    units = weights[0].shape[1]
    wide = jax.ShapeDtypeStruct((shares * rows, units), BF16)
    terms = (
        jax.ShapeDtypeStruct((rows, depth), F32),
        jax.ShapeDtypeStruct((shares - 1, rows, depth), BF16),
    )
    out_shape = terms + (wide,) * len(weights) + (terms if forward else ())
    return pl.pallas_call(
        functools.partial(feed_back_kernel, layer, shares, len(weights) // 3, forward),
        out_shape=out_shape,
        in_specs=[VMEM()] * (2 * shares) + [pl.BlockSpec(memory_space=pl.ANY)] * len(weights),
        out_specs=(VMEM(),) * len(out_shape),
        scratch_shapes=held_weights(weights),
        compiler_params=compiler_params(),
        cost_estimate=cost(
            flops=4 * shares * rows * units * len(weights) * depth,
            bytes_accessed=2 * units * len(weights) * depth,
            transcendentals=shares * rows * units,
        ),
        name="feed_backward",
    )(*blocks, *grads, *weights)


def feed_weights_kernel(shares, added, blocks, *refs):
    refs = list(refs)
    places = refs.pop(0) if blocks else None
    hidden, gate_back, up_back = (refs.pop(0)[...] for _ in range(3))
    mixed = jnp.concatenate([refs.pop(0)[...] for _ in range(shares)], axis=0)
    grads = jnp.concatenate([refs.pop(0)[...] for _ in range(shares)], axis=0)
    received = refs.pop(0) if added else None
    units = hidden.shape[1]
    half = 3 * units // 2
    for index, (left, right) in enumerate(((gate_back, mixed), (up_back, mixed), (hidden, grads))):
        start = index * units
        term = lax.dot_general(left, right, TN, preferred_element_type=F32)
        if added:
            term = term + received[start : start + units, :].astype(F32)
        term = term.astype(BF16)
        if not blocks:
            refs[0][start : start + units, :] = term
            continue
        size = term.shape[1] // blocks
        for part in range(2):
            low, high = max(start, part * half), min(start + units, (part + 1) * half)
            if low >= high:
                continue
            for block in range(blocks):
                piece = term[low - start : high - start, block * size : (block + 1) * size]
                refs[part][block ^ places[part], low - part * half : high - part * half, :] = piece


def feed_weights(activations, mixed, grads, received, places=None, blocks=0):
    shares = len(mixed)
    units = activations[0].shape[1]
    rows, depth = mixed[0].shape
    operands = [*activations, *mixed, *grads] + ([] if received is None else [received])
    specs = [VMEM()] * len(operands)
    if blocks:
        operands = [places] + operands
        specs = [SMEM()] + specs
        out = jax.ShapeDtypeStruct((blocks, 3 * units // 2, depth // blocks), BF16)
        out_shape, out_specs = (out, out), (VMEM(), VMEM())
    else:
        out_shape, out_specs = jax.ShapeDtypeStruct((3 * units, depth), BF16), VMEM()
    return pl.pallas_call(
        functools.partial(feed_weights_kernel, shares, received is not None, blocks),
        out_shape=out_shape,
        in_specs=specs,
        out_specs=out_specs,
        compiler_params=compiler_params(),
        cost_estimate=cost(
            flops=6 * shares * rows * units * depth,
            bytes_accessed=6 * units * depth,
            transcendentals=0,
            scale=WIDE,
        ),
        name="feed_weight_grads",
    )(*operands)


def place_kernel(units, places, *refs):
    parts = refs[:-3]
    outs = refs[-3:]
    parts = [part[0] if len(part.shape) == 3 else part[...] for part in parts if part is not None]
    rows = jnp.concatenate(parts, axis=0).astype(F32)
    for n, out in enumerate(outs):
        out[0] = rows[n * units : (n + 1) * units]


def place_feed(places, parts, blocks, layer, layers, previous):
    depth = blocks * (parts[0].shape[-1] if parts[0].ndim == 3 else parts[0].shape[-1] // blocks)
    units = sum(part.shape[-2] for part in parts) // 3
    size = depth // blocks
    out = jax.ShapeDtypeStruct((layers, units, depth), F32)

    def spec(index, part):
        if part.ndim == 2:
            return pl.BlockSpec((part.shape[0], size), lambda block, places: (0, block))
        return pl.BlockSpec(
            (1, part.shape[1], size), lambda block, places: (block ^ places[index], 0, 0)
        )

    def body(places, *refs):
        place_kernel(units, places, *refs[: len(parts)], *refs[-3:])

    return pl.pallas_call(
        body,
        out_shape=(out,) * 3,
        grid_spec=pltpu.PrefetchScalarGridSpec(
            num_scalar_prefetch=1,
            grid=(blocks,),
            in_specs=[spec(n, part) for n, part in enumerate(parts)]
            + [pl.BlockSpec(memory_space=pl.ANY)] * len(previous),
            out_specs=[pl.BlockSpec((1, units, size), lambda block, places: (layer, 0, block))]
            * 3,
        ),
        input_output_aliases={1 + len(parts) + n: n for n in range(len(previous))},
        compiler_params=compiler_params(),
        name="place_feed_grads",
    )(places, *parts, *previous)


def head_weights_kernel(raws, *refs):
    out = refs[-1]
    rows = jnp.concatenate([ref[...] for ref in refs[:-1]], axis=0)
    left = raws[...].reshape(rows.shape[0], raws.shape[-1])
    out[...] = lax.dot_general(left, rows, TN, preferred_element_type=F32).astype(BF16)


def head_weights(raws, blocks):
    rows, depth = blocks[0].shape
    wide = raws.shape[-1]
    return pl.pallas_call(
        head_weights_kernel,
        out_shape=jax.ShapeDtypeStruct((wide, depth), BF16),
        in_specs=[VMEM()] * (1 + len(blocks)),
        out_specs=VMEM(),
        compiler_params=compiler_params(),
        cost_estimate=cost(
            flops=2 * len(blocks) * rows * wide * depth,
            bytes_accessed=2 * len(blocks) * rows * (wide + depth),
            transcendentals=0,
            scale=WIDE,
        ),
        name="head_weight_grads",
    )(raws, *blocks)


def attend_kernel(chips, rows, width, *refs):
    ids, queries, keys, values, attended, log_totals = refs
    heads = width // HEAD_DIM
    count = 2 * chips * rows
    units = max(count // SEQ_UNIT, 1)
    unit_rows = count // units
    for block in range(2 * chips):
        first = block * rows
        own_unit = first // unit_rows
        segments = [(unit * unit_rows, unit_rows, unit, False) for unit in range(own_unit)]
        if first > own_unit * unit_rows:
            segments.append((own_unit * unit_rows, first - own_unit * unit_rows, None, False))
        segments.append((first, rows, None, True))
        query_all = queries[first : first + rows, :]
        outs = None
        lane = lax.broadcasted_iota(jnp.int32, (rows, 128), 1)
        totals_wide = jnp.zeros((rows, 128), F32)
        for head in range(heads):
            query = head_masked(query_all, head)
            scores, biases, tops = [], [], []
            for start, length, unit, diagonal in segments:
                score = lax.dot_general(
                    query, keys[start : start + length, :], NT, preferred_element_type=F32
                )
                if diagonal:
                    row = lax.broadcasted_iota(jnp.int32, score.shape, 0)
                    column = lax.broadcasted_iota(jnp.int32, score.shape, 1)
                    score = jnp.where(column <= row, score, NEG_LARGE)
                bias = 0.0
                if unit is not None:
                    bias = jnp.where(ids[2 + own_unit * units + unit] > 0, 0.0, NEG_LARGE)
                scores.append(score)
                biases.append(bias)
                tops.append(jnp.max(score, axis=1, keepdims=True) + bias)
            highest = functools.reduce(jnp.maximum, tops)
            summed, total = None, None
            for (start, length, unit, diagonal), score, bias in zip(segments, scores, biases):
                weight = jnp.exp(score - (highest - bias))
                narrow = weight.astype(BF16)
                value = values[start : start + length, :]
                if heads > 1:
                    value_lane = lax.broadcasted_iota(jnp.int32, value.shape, 1)
                    value = jnp.where(value_lane // HEAD_DIM == head, value, jnp.ones_like(value))
                else:
                    part_total = jnp.sum(weight, axis=1, keepdims=True)
                    total = part_total if total is None else total + part_total
                product = jnp.dot(narrow, value, preferred_element_type=F32)
                summed = product if summed is None else summed + product
            if heads > 1:
                spread = pltpu.roll(summed, HEAD_DIM, 1)
                divided = head_masked(summed / spread, head)
                total = jnp.where(lane // HEAD_DIM == head, spread, summed)
                logs = highest + jnp.log(total)
            else:
                divided = summed / total
                logs = jnp.broadcast_to(highest + jnp.log(total), (rows, 128))
            outs = divided if outs is None else outs + divided
            totals_wide = jnp.where(lane == head, logs, totals_wide)
        attended[(block % chips) ^ ids[0], (block // chips) ^ ids[1]] = outs.astype(BF16)
        log_totals[:, first : first + rows] = totals_wide.T[:8]


def attend(ids, queries, keys, values, chips, rows):
    count, width = queries.shape
    heads = width // HEAD_DIM
    pairs = count * count // 2
    return pl.pallas_call(
        functools.partial(attend_kernel, chips, rows, width),
        out_shape=(
            jax.ShapeDtypeStruct((chips, 2, rows, width), BF16),
            jax.ShapeDtypeStruct((8, count), F32),
        ),
        in_specs=[SMEM()] + [VMEM()] * 3,
        out_specs=(VMEM(),) * 2,
        compiler_params=compiler_params(),
        cost_estimate=cost(
            flops=heads * pairs * 256 * 8,
            bytes_accessed=2 * count * width * 4,
            transcendentals=heads * pairs,
        ),
        name="attend_forward",
    )(ids, queries, keys, values)


def attend_back_kernel(chips, rows, width, layer_first, *refs):
    refs = list(refs)
    ids, queries, keys, values, attended = (refs.pop(0) for _ in range(5))
    near = [refs.pop(0) for _ in range(chips)]
    far, log_totals, cosine, sine, weights = (refs.pop(0) for _ in range(5))
    later_layer = refs.pop(0) if layer_first else None
    outs, mine, others, grad_rows, inner, query_total, key_total, value_total = refs
    heads = width // HEAD_DIM
    count = 2 * chips * rows
    units = max(count // SEQ_UNIT, 1)
    unit_rows = count // units

    for core in range(2):
        for chip in range(chips):
            at = place_of(ids, core, chip, chips, rows)
            grad = near[chip][0] if core == 0 else far[chip]
            grad_rows[at, :] = grad
            query_total[at, :] = grad.astype(F32) * attended[chip, core].astype(F32)
    turned = query_total[...].T
    for head in range(heads):
        inner[head : head + 1, :] = jnp.sum(
            turned[head * HEAD_DIM : (head + 1) * HEAD_DIM], axis=0, keepdims=True
        )
    query_total[...] = jnp.zeros_like(query_total)
    key_total[...] = jnp.zeros_like(key_total)
    value_total[...] = jnp.zeros_like(value_total)

    def work(key_start, key_count, query_start, diagonal):
        at = pl.ds(key_start, key_count)
        query_at = pl.ds(query_start, rows)
        key, value = keys[at, :], values[at, :]
        key_part, value_part, query_part = None, None, None
        for head in range(heads):
            query = head_masked(queries[query_at, :], head)
            grad = head_masked(grad_rows[query_at, :], head)
            score = lax.dot_general(key, query, NT, preferred_element_type=F32)
            weight = jnp.exp(score - log_totals[head : head + 1, query_at])
            if diagonal:
                row = lax.broadcasted_iota(jnp.int32, score.shape, 0)
                column = lax.broadcasted_iota(jnp.int32, score.shape, 1)
                weight = jnp.where(row <= column, weight, 0.0)
            back = lax.dot_general(value, grad, NT, preferred_element_type=F32)
            score_back = (weight * (back - inner[head : head + 1, query_at])).astype(BF16)
            narrow = weight.astype(BF16)
            value_term = jnp.dot(narrow, grad, preferred_element_type=F32)
            key_term = jnp.dot(score_back, query, preferred_element_type=F32)
            query_term = lax.dot_general(
                score_back, head_masked(key, head), TN, preferred_element_type=F32
            )
            if head == 0:
                key_part, value_part, query_part = key_term, value_term, query_term
            else:
                key_part, value_part, query_part = (
                    key_part + key_term, value_part + value_term, query_part + query_term,
                )
        key_total[at, :] += key_part
        value_total[at, :] += value_part
        query_total[query_at, :] += query_part

    for unit in range(units):
        start = unit * unit_rows
        blocks = unit_rows // rows
        for other in range(unit):
            @pl.when(ids[2 + unit * units + other] > 0)
            def _():
                @pl.loop(0, blocks)
                def _(index):
                    at = pl.multiple_of(start + index * rows, rows)
                    work(other * unit_rows, unit_rows, at, False)
        for index in range(blocks):
            if index:
                work(start, index * rows, start + index * rows, False)
            work(start + index * rows, rows, start + index * rows, True)

    for core in range(2):
        for chip in range(chips):
            at = place_of(ids, core, chip, chips, rows)
            turn_at = table_rows(ids, core, chip, chips, rows)
            cos, sin = cosine[turn_at, :], sine[turn_at, :]
            query = query_total[at, :] * HEAD_DIM**-0.5
            key = key_total[at, :]
            value = value_total[at, :]
            query = query * cos - half_turn(query) * sin
            key = key * cos - half_turn(key) * sin
            if layer_first:
                value = value + later_layer[core, chip, :, 2 * width :].astype(F32)
            else:
                value = value.astype(BF16).astype(F32) * 0.5
            raws = jnp.concatenate([query, key, value], axis=1).astype(BF16)
            outs[core, chip] = raws
            term = jnp.dot(raws, weights[: 3 * width, :], preferred_element_type=F32)
            if core:
                others[chip] = term.astype(BF16)
            else:
                mine[chip] = term


def attend_back(
    ids, queries, keys, values, attended, near, far, log_totals, cosine, sine, weights, later_layer
):
    chips, _, rows, width = attended.shape
    count = queries.shape[0]
    heads = width // HEAD_DIM
    pairs = count * count // 2
    operands = [ids, queries, keys, values, attended, *near, far, log_totals, cosine, sine, weights]
    depth = weights.shape[1]
    if later_layer is not None:
        operands.append(later_layer)
    return pl.pallas_call(
        functools.partial(attend_back_kernel, chips, rows, width, later_layer is not None),
        out_shape=(
            jax.ShapeDtypeStruct((2, chips, rows, 3 * width), BF16),
            jax.ShapeDtypeStruct((chips, rows, depth), F32),
            jax.ShapeDtypeStruct((chips, rows, depth), BF16),
        ),
        in_specs=[SMEM()] + [VMEM()] * (len(operands) - 1),
        out_specs=(VMEM(),) * 3,
        scratch_shapes=[
            pltpu.VMEM((count, width), BF16),
            pltpu.VMEM((8, count), F32),
            pltpu.VMEM((count, width), F32),
            pltpu.VMEM((count, width), F32),
            pltpu.VMEM((count, width), F32),
        ],
        compiler_params=compiler_params(),
        cost_estimate=cost(
            flops=heads * pairs * 256 * 20,
            bytes_accessed=2 * count * width * 20,
            transcendentals=heads * pairs,
        ),
        name="attend_backward",
    )(*operands)


def rms_factor(values):
    return lax.rsqrt(jnp.mean(values * values, axis=-1, keepdims=True) + EPSILON)


def normed_rows(values, gain):
    return (values * rms_factor(values) * gain).astype(BF16)


def norm_back(values, gain, back):
    factor = rms_factor(values)
    scaled = back * gain
    mean = jnp.mean(scaled * values, axis=-1, keepdims=True)
    gain_grad = jnp.sum(back * values * factor, axis=0)
    return factor * scaled - values * (factor * factor * factor * mean), gain_grad


def matmul(left, right):
    return jnp.dot(left, right, preferred_element_type=F32)


def matmul_nt(left, right):
    return lax.dot_general(left, right, NT, preferred_element_type=F32)


def matmul_tn(left, right):
    return lax.dot_general(left, right, TN, preferred_element_type=F32)


def flat(blocks):
    return blocks.reshape(-1, blocks.shape[-1])


def per_device(
    head_axes, hid_axes, inputs, cotangent, segments, attn_gain, w_query, w_key, w_value, w_out,
    mlp_gain, w_gate, w_up, w_down,
):
    layers = w_query.shape[0]
    core = hid_axes[-1]
    group_axes = head_axes[1:]
    share_axes = hid_axes[:-1]
    chips = 2 ** len(group_axes)
    rows = inputs.shape[0]
    count = 2 * chips * rows
    width = w_query.shape[2]
    units = max(count // SEQ_UNIT, 1)
    share_at = lax.axis_index(share_axes[0])

    def index_of(axes):
        at = jnp.int32(0)
        for axis in axes:
            at = at * 2 + lax.axis_index(axis)
        return at

    def turn(value):
        return lax.ppermute(value, (head_axes[0], core), TURN)

    unit_axes = ((core,) + group_axes)[: (units - 1).bit_length()]
    number = turn(jnp.broadcast_to(segments[:1], (8, 128)))
    unit_at = index_of(unit_axes)
    def group_ids(number):
        numbers = jnp.stack(
            [number] + [swap(number, axes_of(i, unit_axes)) for i in range(1, units)]
        )[:, 0, 0]
        numbers = jnp.stack(
            [lax.dynamic_index_in_dim(numbers, unit ^ unit_at, 0, False) for unit in range(units)]
        )
        same = (numbers[:, None] == numbers[None, :]).astype(jnp.int32)
        places = jnp.stack([index_of(group_axes), lax.axis_index(core)]).astype(jnp.int32)
        earlier_units = np.tril(np.ones((units, units), np.int32), -1)
        starts = jnp.sum(same * earlier_units, axis=1) * SEQ_UNIT
        return jnp.concatenate([places, same.reshape(-1), starts])

    feed_orders = (head_axes[::-1], (head_axes[1], *head_axes[:1:-1], head_axes[0]))
    feed_places = jnp.stack([index_of(order) for order in feed_orders]).astype(jnp.int32)
    frequency = np.float32(THETA) ** (-np.arange(HEAD_DIM // 2, dtype=np.float32) * 2 / HEAD_DIM)
    frequency = np.tile(frequency.astype(np.float32), 2 * width // HEAD_DIM)[None]
    signs = np.where(np.arange(width) % HEAD_DIM < HEAD_DIM // 2, -1.0, 1.0).astype(np.float32)
    angles = jnp.arange(count, dtype=jnp.int32).astype(F32)[:, None] * frequency
    cosine, sine = jnp.cos(angles), jnp.sin(angles) * signs

    feed_all = (w_gate.transpose(0, 2, 1), w_up.transpose(0, 2, 1), w_down)

    def joined_shares(piece):
        other = swap(piece, share_axes[:1])
        return jnp.where(
            share_at == 0,
            jnp.concatenate([piece, other], axis=0),
            jnp.concatenate([other, piece], axis=0),
        )

    packed = pack_heads(share_at[None].astype(jnp.int32), (w_query, w_key, w_value, w_out))

    def summed_shares(part):
        kept = lax.dynamic_slice_in_dim(part, share_at * 2 * width, 2 * width, 0)
        sent = lax.dynamic_slice_in_dim(part, (1 - share_at) * 2 * width, 2 * width, 0)
        return (kept.astype(F32) + swap(sent, share_axes[:1]).astype(F32)).astype(BF16)

    def add_received(total, sent):
        for i in range(1, 1 + sent.shape[0]):
            total = total + swap(sent[i - 1], axes_of(i, share_axes)).astype(F32)
        return total

    attn_gains = [attn_gain[n][None] for n in range(layers)]
    mlp_gains = [mlp_gain[n][None] for n in range(layers)]
    residual = turn(inputs)
    w_heads = [turn(packed[0])] + [None] * (layers - 1)
    residual, cosine, sine = lax.optimization_barrier((residual, cosine, sine))
    residual = residual.astype(F32)
    w_outs = [None] * layers

    stored = []
    first_values = None
    for layer in range(layers):
        final = layer == layers - 1
        before = residual
        normed = normed_rows(before, attn_gains[layer])
        if layer == 0:
            near, far = gather(normed, group_axes, core, w_heads[0])
            w_heads[0] = joined_shares(w_heads[0])
        else:
            w_heads[layer] = joined_shares(after(w_heads[layer], before))
            near, far = gather(normed, group_axes, core, w_heads[layer])
        blocks = near + far
        if layer == 0:
            ids = group_ids(after(number, near[1]))
        queries, keys, values = project(ids, blocks, w_heads[layer], cosine, sine, first_values)
        if layer == 0:
            first_values = values
            feeds = [swap(after(feed_all[0], queries), (core,))]
        out_chips = gather_chips(after(w_heads[layer][3 * width :], queries), group_axes)
        attended, log_totals = attend(ids, queries, keys, values, chips, rows)
        attended = after(attended, *out_chips[1:], *(feeds if layer == 0 else ()))
        out_chips = jnp.concatenate(out_chips, axis=0)
        w_outs[layer] = jnp.concatenate([out_chips, swap(out_chips, (core,))], axis=0)
        if layer == 1:
            down_in = gather_chips(after(grad, queries), share_axes)
            attended = after(attended, down_in[-1])
        near, far = exchange(attended, group_axes, core)
        if layer == 0:
            feeds += [swap(after(w, far, w_outs[0]), (core,)) for w in feed_all[1:]]
            feed_all = feed_all + tuple(feeds)
            grad = turn(after(cotangent, far))
        attended_rows, middle, normed = middle_step(
            near, far, w_outs[layer], before, mlp_gains[layer]
        )
        mixed = gather_chips(normed, share_axes)
        stored.append(
            dict(
                before=before, blocks=blocks, queries=queries, keys=keys, values=values,
                attended=attended, log_totals=log_totals, attended_rows=attended_rows,
                middle=middle, mixed=mixed,
            )
        )
        if not final:
            w_heads[layer + 1] = turn(after(packed[layer + 1], far))
            first_mixed = after(mixed[0], w_heads[layer + 1])
            own_term, sent = feed_forward(layer, [first_mixed] + mixed[1:], feed_all)
            residual = add_received(middle + own_term, sent)
            if layer == 0:
                residual = after(residual, grad)

    grad = grad.astype(F32)
    attn_parts, mlp_grads = [], []
    attn_gain_grads, mlp_gain_grads = [], []
    later_layer, sums = None, []
    by_blocks = inputs.shape[1] % (128 * 2 ** len(head_axes)) == 0
    for layer in reversed(range(layers)):
        final = layer == layers - 1
        k = stored[layer]
        mixed = k["mixed"]
        if not final:
            down_in = gather_chips(grad.astype(BF16), share_axes)
            if by_blocks:
                mixed = [after(mixed[0], sums[0][0].step())] + mixed[1:]
        own_term, sent, *rest = feed_back(layer, mixed, down_in, feed_all, final)
        received = [swap(sent[i - 1], axes_of(i, share_axes)) for i in range(1, len(mixed))]
        if not final and by_blocks:
            rest[3] = after(rest[3], sums[0][1].step())
        other = swap(feed_weights(rest[3:6], mixed, down_in, None), (core,))
        if not final and by_blocks:
            other = after(other, *steps(sums[0]))
        if by_blocks:
            mlp_part = feed_weights(
                rest[:3], mixed, down_in, other, feed_places, 2 ** len(head_axes)
            )
            sums.insert(0, [BlockSum(p, order) for p, order in zip(mlp_part, feed_orders)])
        else:
            mlp_part = (feed_weights(rest[:3], mixed, down_in, other),)
            mlp_grads.insert(0, lax.psum(mlp_part[0], head_axes if layer else head_axes[::-1]))
        middle_back, attn_in, gain_part, heads_back = middle_back_step(
            own_term, received, k["middle"], mlp_gains[layer], w_outs[layer], grad, chips
        )
        mlp_gain_grads.append(gain_part[0])
        near, far = exchange(heads_back, group_axes, core)
        if by_blocks and layer == 0:
            far = after(far, *steps(sums[0]))
        if final:
            block_out = add_received(k["middle"] + rest[6], after(rest[7], far)).astype(BF16)
        raws, mine, others = attend_back(
            ids, k["queries"], k["keys"], k["values"], k["attended"], near, far,
            k["log_totals"], cosine, sine, w_heads[layer], later_layer,
        )
        later_layer = raws
        if by_blocks:
            others = after(others, *steps(sums[0]))
        if final:
            others, block_out = lax.optimization_barrier((others, block_out))
        if layer == layers - 2:
            block_out = turn(after(block_out, far))
            others, block_out = lax.optimization_barrier((others, block_out))
        ties = steps(sums[0]) if by_blocks and layer else ()
        normed_in = scatter_sum(mine, others, group_axes, core, *ties)
        part, gain_part = norm_back(k["before"], attn_gains[layer], normed_in)
        attn_gain_grads.append(gain_part)
        grad = middle_back + part
        if by_blocks:
            grad = after(grad, *steps(sums[0]))
        attn_parts.insert(0, (raws, attn_in))

    out_terms = jnp.stack(
        [
            matmul_tn(stored[n]["attended_rows"], after(attn_in, grad) if n else attn_in).reshape(
                2, chips, width, -1
            )
            for n, (_, attn_in) in enumerate(attn_parts)
        ],
        axis=2,
    )
    out_terms, grad = lax.optimization_barrier((out_terms, grad))
    mine = out_terms[0] + swap(out_terms[1].astype(BF16), (core,)).astype(F32)
    sent = mine.astype(BF16)
    ties = steps(sums[0], sent) + steps(sums[1], sent) if by_blocks else ()
    out_grads = mine[0]
    for i in range(1, chips):
        out_grads = out_grads + swap(sent[i], axes_of(i, group_axes)).astype(F32)
    out_grads = out_grads.astype(BF16)
    heads_grads = [
        head_weights(after(raws, grad, *([] if n else ties[:2])), stored[n]["blocks"])
        for n, (raws, _) in enumerate(attn_parts)
    ]
    sixth = ties[2:]
    ties = steps(sums[0], out_grads) if by_blocks else ()
    late = steps(sums[0]) + sixth if by_blocks else ()

    gains = jnp.stack(attn_gain_grads[::-1] + mlp_gain_grads[::-1])
    gains = exchange_sum(gains, hid_axes[::-1] + head_axes, F32)
    part = [jnp.concatenate(pair, axis=0) for pair in zip(heads_grads, out_grads)]
    part = summed_shares(jnp.stack(part, axis=1))
    part, gains, *_ = lax.optimization_barrier((part, gains, *ties))
    part = turn(part)
    given = grad.astype(BF16)
    part, given, *_ = lax.optimization_barrier((part, given, *late))
    given = turn(given).astype(F32)
    part = exchange_sum(part, (core,) + share_axes[1:])
    attn_all = joined_shares(part).astype(F32).transpose(1, 0, 2)

    if by_blocks:
        feed_grads = ()
        for layer in reversed(range(layers)):
            while sums[layer][0].done < 2 * len(head_axes):
                steps(sums[layer])
            feed_grads = place_feed(
                feed_places, [part.kept for part in sums[layer]], 2 ** len(head_axes), layer, layers, feed_grads
            )
    else:
        mlp_all = jnp.stack(mlp_grads).astype(F32)
        size = w_gate.shape[2]
        feed_grads = [mlp_all[:, n * size : (n + 1) * size] for n in range(3)]
    return (
        block_out,
        given,
        gains[:layers],
        attn_all[:, :width].transpose(0, 2, 1),
        attn_all[:, width : 2 * width].transpose(0, 2, 1),
        attn_all[:, 2 * width : 3 * width].transpose(0, 2, 1),
        attn_all[:, 3 * width :],
        gains[layers:],
        feed_grads[0].transpose(0, 2, 1),
        feed_grads[1].transpose(0, 2, 1),
        feed_grads[2],
    )


def solution(mesh):
    head_bits = (mesh.shape["heads"] - 1).bit_length()
    hid_bits = (mesh.shape["hid"] - 1).bit_length()
    head_axes = tuple(f"heads{n}" for n in range(head_bits))
    hid_axes = tuple(f"hid{n}" for n in range(hid_bits))
    binary = Mesh(mesh.devices.reshape((2,) * (head_bits + hid_bits)), head_axes + hid_axes)
    tokens = hid_axes + head_axes
    in_specs = (
        P(tokens, None),
        P(tokens, None),
        P(tokens),
        P(),
        P(None, None, head_axes),
        P(None, None, head_axes),
        P(None, None, head_axes),
        P(None, head_axes, None),
        P(),
        P(None, None, hid_axes),
        P(None, None, hid_axes),
        P(None, hid_axes, None),
    )
    out_specs = (
        P(tokens, None),
        P(tokens, None),
        P(),
        P(None, None, head_axes),
        P(None, None, head_axes),
        P(None, None, head_axes),
        P(None, head_axes, None),
        P(),
        P(None, None, hid_axes),
        P(None, None, hid_axes),
        P(None, hid_axes, None),
    )
    return jax.shard_map(
        functools.partial(per_device, head_axes, hid_axes),
        mesh=binary,
        in_specs=in_specs,
        out_specs=out_specs,
        check_vma=False,
    )
```
